128 devices in a mesh: ctx: 16 (over y, x_lo, core), section: 8 (over z, x_hi).
Axes of the slice: x: 4 (x_hi: 2, x_lo: 2; x = x_hi * 2 + x_lo), y: 4, z: 4, core: 2. Of those that a mesh axis runs over, the one named last changes fastest.
Arguments:
- x_saved: bfloat16 [8, 2048, 4096], P('section', 'ctx'), may hold values from -400 to 400
- gains: float32 [8, 4096], P('section'), may hold values from 0.5 to 2
- keys: bfloat16 [2048, 4096], P(('ctx', 'section')), may hold values from -18 to 18
- values: bfloat16 [2048, 4096], P(('ctx', 'section')), may hold values from -6 to 6
- grad_top: bfloat16 [2048, 4096], P('ctx'), may hold values from -6 to 6
- block_order: int32 [16], replicated, may hold values from 0 to 15, each once
Outputs:
- grad_inputs: float32 [8, 2048, 4096], P('section', 'ctx')
- grad_keys: float32 [2048, 4096], P(('ctx', 'section'))
- grad_values: float32 [2048, 4096], P(('ctx', 'section'))
The draws below stay inside these ranges and needn't reach their ends.
Inputs may be any that keep to these rules, and one draw needn't show every extreme that they name: `block_order`: each place occurs once.
All inputs are finite; a program needn't handle non-finite values.
Results may differ from the reference program's by a relative error of at most 0.015.
The reference program's roundings to bfloat16 on the way count: a program that leaves them out, or rounds other values in their place, can miss the bound.
Values may be sent and summed in bfloat16 or wider, within the bound.
A program may use at most 128 MiB of HBM per device.

```python
import math
from functools import partial
import jax
import jax.numpy as jnp
from jax import lax

H = 32
HD = 128
TOK_DEV = 128
LAYERS = 8
WIDTH = 4096
TOKENS = 2048
N_CTX = 16


def draw_x_saved(key, part):
    key = jax.random.fold_in(key, 11)
    first, second, third = jax.random.split(key, 3)
    row_scale = jnp.exp(jax.random.uniform(first, (LAYERS, TOKENS, 1), jnp.float32, 0.0, math.log(10.0)))
    col_scale = jnp.exp(jax.random.uniform(second, (1, 1, WIDTH), jnp.float32, 0.0, math.log(10.0)))
    base = jax.random.truncated_normal(third, -4.0, 4.0, (LAYERS, TOKENS, WIDTH), jnp.float32)
    filled = base * row_scale * col_scale
    return filled.astype(jnp.bfloat16)


def draw_keys(key, part):
    key = jax.random.fold_in(key, 12)
    base = 1.5 * jax.random.truncated_normal(key, -6.0, 6.0, (TOKENS, WIDTH), jnp.float32)
    return base.astype(jnp.bfloat16)


def level_of(key, dims, cuts, least, top_value):
    def one(position, blocks):
        steps = jax.random.uniform(jax.random.fold_in(jax.random.fold_in(key, 6), position), (blocks,), jnp.float32, least / len(cuts), top_value / len(cuts))
        return jnp.repeat(jnp.exp(steps), dims[position] // blocks).reshape((-1,) + (1,) * (len(dims) - position - 1))

    factor_of = one(*cuts[0])
    for cut in cuts[1:]:
        factor_of = factor_of * one(*cut)
    return factor_of


def scatter_about(rng, shape, width, bound, pieces=(), kind=jnp.bfloat16):
    drawn = jax.random.normal(rng, shape, jnp.float32) * width
    if len(pieces) > 0:
        drawn = level_of(rng, shape, pieces, -0.22, 0.18) * drawn
    return jnp.clip(drawn, min=-bound, max=bound).astype(kind)


def setup_inputs(seed: int = 0) -> dict:
    arg_keys = jax.random.split(jax.random.key(seed), 7)
    x_saved = draw_x_saved(jax.random.fold_in(arg_keys[6], 71), 0)
    gains = jnp.clip(jnp.exp(math.log(2.0) - 1.3862944 * jax.random.uniform(arg_keys[1], (LAYERS, WIDTH), jnp.float32) ** level_of(arg_keys[1], (LAYERS, WIDTH), ((0, 8),), -0.2, 0.2)), 0.5, 2.0)
    keys = draw_keys(jax.random.fold_in(arg_keys[6], 71), 0)
    values = scatter_about(arg_keys[3], (TOKENS, WIDTH), 1.0, 6.0, ((0, 128),))
    grad_top = scatter_about(arg_keys[4], (TOKENS, WIDTH), 1.0, 6.0, ((0, 16),))
    block_order = jax.random.permutation(arg_keys[5], N_CTX).astype(jnp.int32)
    return dict(x_saved=x_saved, gains=gains, keys=keys, values=values, grad_top=grad_top, block_order=block_order)


masked_score = -1e+30
norm_eps = 1e-06

def make_query(inputs, gain_row):
    x_float = inputs.astype(jnp.float32).reshape(inputs.shape[0], H, HD)
    inv_rms = lax.rsqrt(lax.optimization_barrier(jnp.mean(x_float * x_float, axis=-1, keepdims=True)) + norm_eps)
    queries = x_float * inv_rms * gain_row.astype(jnp.float32).reshape(H, HD)
    return (queries, x_float, inv_rms)

def input_grad(query_grads, x_float, inv_rms, gain_row):
    scaled = query_grads * gain_row.astype(jnp.float32).reshape(H, HD)
    inner = lax.optimization_barrier(jnp.mean(scaled * x_float, axis=-1, keepdims=True))
    result = inv_rms * scaled - x_float * (inv_rms * inv_rms * inv_rms) * inner
    return result.reshape(query_grads.shape[0], H * HD)

def head_backward(operands, visible):
    query_low, key_head, value_head, grad_low = operands
    q_float = query_low.astype(jnp.float32)
    k_float = key_head.astype(jnp.float32)
    v_float = value_head.astype(jnp.float32)
    g_float = grad_low.astype(jnp.float32)
    factor = 1.0 / math.sqrt(HD)
    scores = jnp.dot(q_float, k_float.T) * factor
    scores = jnp.where(visible, scores, masked_score)
    row_max = lax.optimization_barrier(jnp.max(scores, axis=-1, keepdims=True))
    probs = jnp.exp(scores - row_max)
    probs = probs / lax.optimization_barrier(jnp.sum(probs, axis=-1, keepdims=True))
    probs_low = lax.optimization_barrier(probs.astype(jnp.bfloat16)).astype(jnp.float32)
    recomputed = jnp.dot(probs_low, v_float)
    row_delta = lax.optimization_barrier(jnp.sum(g_float * recomputed, axis=-1))
    dprobs = jnp.dot(g_float, v_float.T)
    dscores = probs * (dprobs - row_delta[:, None])
    dscores = lax.optimization_barrier(dscores.astype(jnp.bfloat16)).astype(jnp.float32)
    query_grad = jnp.dot(dscores, k_float) * factor
    key_part = jnp.dot(dscores.T, q_float) * factor
    value_part = jnp.dot(probs_low.T, g_float)
    return (query_grad, key_part, value_part)

def reference(x_saved, gains, keys, values, grad_top, block_order):
    places = (block_order[:, None] * TOK_DEV + jnp.arange(TOK_DEV, dtype=jnp.int32)[None, :]).reshape(TOKENS)
    visible = places[:, None] >= places[None, :]
    keys_split = keys.reshape(TOKENS, H, HD).transpose(1, 0, 2)
    values_split = values.reshape(TOKENS, H, HD).transpose(1, 0, 2)
    incoming = grad_top.astype(jnp.float32)
    key_total = jnp.zeros((TOKENS, H * HD), jnp.float32)
    value_total = jnp.zeros((TOKENS, H * HD), jnp.float32)
    layer_grads = []
    for layer_id in range(LAYERS - 1, -1, -1):
        queries, x_float, inv_rms = make_query(x_saved[layer_id], gains[layer_id])
        query_low = queries.astype(jnp.bfloat16).transpose(1, 0, 2)
        grad_low = incoming.astype(jnp.bfloat16).reshape(TOKENS, H, HD).transpose(1, 0, 2)
        query_grads, key_part, value_part = lax.map(partial(head_backward, visible=visible), (query_low, keys_split, values_split, grad_low))
        incoming = incoming + input_grad(query_grads.transpose(1, 0, 2), x_float, inv_rms, gains[layer_id])
        layer_grads.append(incoming)
        key_total = key_total + key_part.transpose(1, 0, 2).reshape(TOKENS, H * HD)
        value_total = value_total + value_part.transpose(1, 0, 2).reshape(TOKENS, H * HD)
    return (jnp.stack(layer_grads[::-1]), key_total, value_total)
```

```python
import functools
import math

import jax
import jax.numpy as jnp
from jax import lax
from jax.experimental import pallas as pl
from jax.experimental.pallas import tpu as pltpu
from jax.sharding import PartitionSpec as P

H = 32
HD = 128
LAYERS = 8
N_CTX = 16
TOK_DEV = 128
HEADS_SEC = 4
QUARTERS = 4
ROWS = TOK_DEV // QUARTERS
NQ = N_CTX * ROWS
NK = N_CTX * TOK_DEV
CHUNKS = 4
CK = NK // CHUNKS
CQ = NQ // CHUNKS

masked_score = -1e30
norm_eps = 1e-06
factor = 1.0 / math.sqrt(HD)
log2e = math.log2(math.e)

NT = (((1,), (1,)), ((), ()))
NN = (((1,), (0,)), ((), ()))


def dot(a, b, dims):
    return lax.dot_general(a, b, dims, preferred_element_type=jnp.float32)


def attend_kernel(
    place_ref,
    block_ref,
    x_ref,
    gain_ref,
    k_in,
    v_in,
    top_ref,
    g_out,
    dk_out,
    dv_out,
    k_ref,
    v_ref,
    kt_ref,
    s_ref,
    dp_ref,
    g_ref,
    dk_ref,
    dv_ref,
):
    quarter = lax.axis_index("ctx") % QUARTERS
    for p in range(N_CTX):
        b = block_ref[p]
        k_ref[p * TOK_DEV : (p + 1) * TOK_DEV, :] = k_in[b]
        v_ref[p * TOK_DEV : (p + 1) * TOK_DEV, :] = v_in[b]
        g_ref[p * ROWS : (p + 1) * ROWS, :] = top_ref[b].astype(jnp.float32)
    for j in range(CHUNKS):
        rows = slice(j * CK, (j + 1) * CK)
        kt_ref[:, rows] = jnp.transpose(k_ref[rows, :])
    dk_ref[...] = jnp.zeros_like(dk_ref)
    dv_ref[...] = jnp.zeros_like(dv_ref)

    lane = lax.broadcasted_iota(jnp.int32, (1, CQ), 1)
    query_at = (lane // ROWS) * TOK_DEV + quarter * ROWS + lane % ROWS
    key_at = lax.broadcasted_iota(jnp.int32, (CK, CQ), 0)
    seen = key_at <= query_at

    def one_layer(step, carry):
        layer = LAYERS - 1 - step
        xf = jnp.concatenate(
            [x_ref[block_ref[p], layer] for p in range(N_CTX)], axis=0
        ).astype(jnp.float32)
        gain = gain_ref[pl.ds(layer, 1), :]
        inv_rms = lax.rsqrt(jnp.mean(xf * xf, axis=1, keepdims=True) + norm_eps)
        query = (xf * inv_rms * gain).astype(jnp.bfloat16)
        grad = g_ref[...].astype(jnp.bfloat16)

        tops = []
        for j in range(CHUNKS):
            rows, first = slice(j * CK, (j + 1) * CK), j * CQ
            s = dot(k_ref[rows, :], query[first:, :], NT)
            diag = jnp.where(seen, s[:, :CQ], masked_score)
            s_ref[rows, first : first + CQ] = diag
            top = jnp.max(diag, axis=0, keepdims=True)
            if j < CHUNKS - 1:
                s_ref[rows, first + CQ :] = s[:, CQ:]
                top = jnp.concatenate([top, jnp.max(s[:, CQ:], axis=0, keepdims=True)], axis=1)
            tops.append(top)
        row_max = tops[0]
        for j in range(1, CHUNKS):
            row_max = jnp.concatenate(
                [row_max[:, : j * CQ], jnp.maximum(row_max[:, j * CQ :], tops[j])], axis=1
            )

        def add_from(total, part, first):
            if first == 0:
                return part if total is None else total + part
            return jnp.concatenate([total[:, :first], total[:, first:] + part], axis=1)

        total = None
        for j in range(CHUNKS):
            rows, first = slice(j * CK, (j + 1) * CK), j * CQ
            e = jnp.exp2((s_ref[rows, first:] - row_max[:, first:]) * (factor * log2e))
            s_ref[rows, first:] = e
            total = add_from(total, jnp.sum(e, axis=0, keepdims=True), first)
        inv_total = 1.0 / total

        delta = None
        for j in range(CHUNKS):
            rows, first = slice(j * CK, (j + 1) * CK), j * CQ
            dp = dot(v_ref[rows, :], grad[first:, :], NT)
            dp_ref[rows, first:] = dp
            probs = s_ref[rows, first:] * inv_total[:, first:]
            s_ref[rows, first:] = probs
            low = probs.astype(jnp.bfloat16)
            delta = add_from(
                delta, jnp.sum(low.astype(jnp.float32) * dp, axis=0, keepdims=True), first
            )
            dv_ref[rows, :] += dot(low, grad[first:, :], NN)

        dq_t = None
        for j in range(CHUNKS):
            rows, first = slice(j * CK, (j + 1) * CK), j * CQ
            ds = (s_ref[rows, first:] * (dp_ref[rows, first:] - delta[:, first:])).astype(
                jnp.bfloat16
            )
            dk_ref[rows, :] += dot(ds, query[first:, :], NN)
            dq_t = add_from(dq_t, dot(kt_ref[:, rows], ds, NN), first)
        scaled = jnp.transpose(dq_t) * (gain * factor)
        inner = jnp.mean(scaled * xf, axis=1, keepdims=True)
        g_ref[...] += inv_rms * scaled - xf * (inv_rms * inv_rms * inv_rms) * inner
        for b in range(N_CTX):
            at = pl.ds(pl.multiple_of(place_ref[b] * ROWS, ROWS), ROWS)
            g_out[b, pl.ds(layer, 1)] = g_ref[at, :].astype(jnp.bfloat16)[None]
        return carry

    lax.fori_loop(0, LAYERS, one_layer, 0)
    for b in range(N_CTX):
        at = pl.ds(pl.multiple_of(place_ref[b] * TOK_DEV, TOK_DEV), TOK_DEV)
        dk_out[b] = (dk_ref[at, :] * factor).astype(jnp.bfloat16)
        dv_out[b] = dv_ref[at, :].astype(jnp.bfloat16)


def attend(places, blocks, x, gains, keys, values, top):
    smem = pl.BlockSpec(memory_space=pltpu.SMEM)
    vmem = pl.BlockSpec(memory_space=pltpu.VMEM)
    return pl.pallas_call(
        attend_kernel,
        out_shape=(
            jax.ShapeDtypeStruct((N_CTX, LAYERS, ROWS, HD), jnp.bfloat16),
            jax.ShapeDtypeStruct((N_CTX, TOK_DEV, HD), jnp.bfloat16),
            jax.ShapeDtypeStruct((N_CTX, TOK_DEV, HD), jnp.bfloat16),
        ),
        in_specs=[smem, smem, vmem, vmem, vmem, vmem, vmem],
        out_specs=(vmem, vmem, vmem),
        scratch_shapes=[
            pltpu.VMEM((NK, HD), jnp.bfloat16),
            pltpu.VMEM((NK, HD), jnp.bfloat16),
            pltpu.VMEM((HD, NK), jnp.bfloat16),
            pltpu.VMEM((NK, NQ), jnp.float32),
            pltpu.VMEM((NK, NQ), jnp.float32),
            pltpu.VMEM((NQ, HD), jnp.float32),
            pltpu.VMEM((NK, HD), jnp.float32),
            pltpu.VMEM((NK, HD), jnp.float32),
        ],
        compiler_params=pltpu.CompilerParams(vmem_limit_bytes=56 * 2**20),
    )(places, blocks, x, gains, keys, values, top)


def swap(value, axis):
    return lax.all_to_all(value, axis, split_axis=0, concat_axis=0, tiled=True)


def body(x_saved, gains, keys, values, grad_top, block_order):
    section = lax.axis_index("section")
    head = lax.axis_index("ctx") // QUARTERS
    wide = HEADS_SEC * HD
    n_sec = lax.axis_size("section")
    blocks = jnp.sum(
        jnp.where(
            block_order[None, :] == jnp.arange(N_CTX, dtype=jnp.int32)[:, None],
            jnp.arange(N_CTX, dtype=jnp.int32)[None, :],
            0,
        ),
        axis=1,
        dtype=jnp.int32,
    )

    x = swap(x_saved[0].reshape(TOK_DEV, n_sec, wide).transpose(1, 0, 2), "section")
    x = x.reshape(LAYERS, QUARTERS, ROWS, HEADS_SEC, HD).transpose(3, 1, 0, 2, 4)
    x = swap(x.reshape(N_CTX, LAYERS, ROWS, HD), "ctx")

    def spread(value):
        value = swap(value.reshape(-1, n_sec, wide).transpose(1, 0, 2), "section")
        value = value.reshape(TOK_DEV, HEADS_SEC, 1, HD).transpose(1, 2, 0, 3)
        value = jnp.broadcast_to(value, (HEADS_SEC, QUARTERS, TOK_DEV, HD))
        return swap(value.reshape(N_CTX, TOK_DEV, HD), "ctx")

    k, v = spread(keys), spread(values)
    gain = swap(gains.reshape(n_sec, wide), "section")
    gain = lax.dynamic_slice_in_dim(gain, head * HD, HD, 1)
    top = lax.dynamic_slice_in_dim(grad_top, section * wide, wide, 1)
    top = top.reshape(QUARTERS, ROWS, HEADS_SEC, HD).transpose(2, 0, 1, 3)
    top = swap(top.reshape(N_CTX, ROWS, HD), "ctx")

    g, dk, dv = attend(block_order, blocks, x, gain, k, v, top)

    g = swap(g, "ctx").reshape(HEADS_SEC, QUARTERS, LAYERS, ROWS, HD).transpose(2, 1, 3, 0, 4)
    g = swap(g.reshape(LAYERS, TOK_DEV, wide), "section")
    g = g.transpose(1, 0, 2).reshape(1, TOK_DEV, H * HD).astype(jnp.float32)

    def gather(value):
        value = swap(value, "ctx").reshape(HEADS_SEC, QUARTERS, TOK_DEV, HD)
        value = jnp.sum(value.astype(jnp.float32), axis=1).astype(jnp.bfloat16)
        value = value.transpose(1, 0, 2).reshape(n_sec, TOK_DEV // n_sec, wide)
        value = swap(value, "section")
        return value.transpose(1, 0, 2).reshape(-1, H * HD).astype(jnp.float32)

    return (g, gather(dk), gather(dv))


def solution(mesh):
    placed = (
        P("section", "ctx", None),
        P("section", None),
        P(("ctx", "section"), None),
        P(("ctx", "section"), None),
        P("ctx", None),
        P(),
    )
    return jax.shard_map(
        body,
        mesh=mesh,
        in_specs=placed,
        out_specs=(
            P("section", "ctx", None),
            P(("ctx", "section"), None),
            P(("ctx", "section"), None),
        ),
        check_vma=False,
    )
```

```python
import math

import jax
import jax.numpy as jnp
from jax import lax
from jax.experimental import pallas as pl
from jax.experimental.pallas import tpu as pltpu
from jax.sharding import PartitionSpec as P

H = 32
HD = 128
LAYERS = 8
N_SEC = LAYERS
N_CTX = 16
TOK_DEV = 128
WIDTH = H * HD
HEADS_SEC = H // N_SEC
WIDE = HEADS_SEC * HD
QUARTERS = N_CTX // HEADS_SEC
ROWS = TOK_DEV // QUARTERS
TOK_SEC = TOK_DEV // N_SEC
NQ = N_CTX * ROWS
NK = N_CTX * TOK_DEV
CHUNKS = 4
CK = NK // CHUNKS
CQ = NQ // CHUNKS
LAG = 2

masked_score = -1e30
norm_eps = 1e-06
factor = 1.0 / math.sqrt(HD)
log2e = math.log2(math.e)

NT = (((1,), (1,)), ((), ()))
NN = (((1,), (0,)), ((), ()))
BF16, F32 = jnp.bfloat16, jnp.float32


def dot(a, b, dims):
    return lax.dot_general(a, b, dims, preferred_element_type=jnp.float32)


def add_from(total, part, first):
    if total is None:
        return part
    if first == 0:
        return total + part
    return jnp.concatenate([total[:, :first], total[:, first:] + part], axis=1)


def max_from(total, part, first):
    if total is None:
        return part
    return jnp.concatenate([total[:, :first], jnp.maximum(total[:, first:], part)], axis=1)


def pick(wanted, options):
    chosen = options[0][1]
    for number, option in options[1:]:
        chosen = lax.select(number == wanted, option, chosen)
    return chosen


def cut(index, size):
    return pl.ds(pl.multiple_of(index * size, size), size)


def kernel(
    place_ref,
    x_hbm,
    gain_hbm,
    keys_hbm,
    values_hbm,
    top_hbm,
    grads_out,
    dk_out,
    dv_out,
    k1,
    v1,
    x1,
    gain1,
    top2,
    k2,
    v2,
    x2,
    xw,
    k_ref,
    v_ref,
    kt_ref,
    s_ref,
    dp_ref,
    g_ref,
    dk_ref,
    dv_ref,
    g1,
    y1,
    dk1,
    dv1,
    dk2,
    dv2,
    dk3,
    dv3,
    send,
    recv,
    gain_send,
    gain_recv,
    x1_recv,
    x2_send,
    x2_recv,
    g1_send,
    g1_recv,
    g2_send,
):
    c, s = lax.axis_index("ctx"), lax.axis_index("section")
    head, quarter = c // QUARTERS, c % QUARTERS

    def ctx_at(k):
        y = (c // 4 + k // 4) % 4
        x_lo = (c // 2 + k // 2) % 2
        return y * 4 + x_lo * 2 + (c + k) % 2

    def sec_at(k):
        return ((s // 2 + k // 2) % 4) * 2 + (s + k) % 2

    def away(source, target, send_sem, recv_sem, device):
        return pltpu.make_async_remote_copy(
            src_ref=source,
            dst_ref=target,
            send_sem=send_sem,
            recv_sem=recv_sem,
            device_id=device,
            device_id_type=pl.DeviceIdType.MESH,
        )

    def wait_for(ref, sem):
        pltpu.make_async_copy(ref, ref, sem).wait()

    def each(count, step):
        def run(k, carry):
            step(k)
            return carry

        lax.fori_loop(1, count, run, 0)

    barrier = pltpu.get_barrier_semaphore()

    def greet_ctx(k):
        pl.semaphore_signal(
            barrier, inc=1, device_id=(ctx_at(k), s), device_id_type=pl.DeviceIdType.MESH
        )

    def greet_sec(k):
        pl.semaphore_signal(
            barrier, inc=1, device_id=(c, sec_at(k)), device_id_type=pl.DeviceIdType.MESH
        )

    each(N_SEC, greet_sec)
    each(N_CTX, greet_ctx)
    pl.semaphore_wait(barrier, N_SEC + N_CTX - 2)

    def send_kv1(k):
        to = sec_at(k)
        for n, (source, target) in enumerate(((keys_hbm, k1), (values_hbm, v1))):
            away(
                source.at[:, cut(to, WIDE)],
                target.at[cut(s, TOK_SEC), :],
                send.at[n],
                recv.at[n],
                (c, to),
            ).start()

    each(N_SEC, send_kv1)
    for n, (source, target) in enumerate(((keys_hbm, k1), (values_hbm, v1))):
        pltpu.make_async_copy(
            source.at[:, cut(s, WIDE)], target.at[cut(s, TOK_SEC), :], recv.at[n]
        ).start()

    def send_gain(k):
        to = sec_at(k)
        away(
            gain_hbm.at[:, cut(to * HEADS_SEC + head, HD)],
            gain1.at[s],
            gain_send.at[k],
            gain_recv.at[s],
            (c, to),
        ).start()

    each(N_SEC, send_gain)
    pltpu.make_async_copy(
        gain_hbm.at[:, cut(s * HEADS_SEC + head, HD)], gain1.at[s], gain_recv.at[s]
    ).start()

    def send_x1(k):
        to = sec_at(k)
        away(
            x_hbm.at[0, :, cut(to, WIDE)], x1.at[s], send.at[2], x1_recv.at[s], (c, to)
        ).start()

    each(N_SEC, send_x1)
    pltpu.make_async_copy(x_hbm.at[0, :, cut(s, WIDE)], x1.at[s], x1_recv.at[s]).start()

    def send_top(k):
        to = ctx_at(k)
        away(
            top_hbm.at[cut(to % QUARTERS, ROWS), cut(s * HEADS_SEC + to // QUARTERS, HD)],
            top2.at[c],
            send.at[3],
            recv.at[3],
            (to, s),
        ).start()

    each(N_CTX, send_top)
    pltpu.make_async_copy(
        top_hbm.at[cut(quarter, ROWS), cut(s * HEADS_SEC + head, HD)], top2.at[c], recv.at[3]
    ).start()

    places = [place_ref[b] for b in range(N_CTX)]

    def in_order(ref, target, size, kind):
        blocks = [(places[b], ref[b]) for b in range(N_CTX)]
        for p in range(N_CTX):
            target[p * size : (p + 1) * size, :] = pick(p, blocks).astype(kind)

    def in_blocks(ref, size, target, at):
        sorted_rows = [(p, ref[p * size : (p + 1) * size, :].astype(BF16)) for p in range(N_CTX)]
        for b in range(N_CTX):
            target[(*at, b)] = pick(places[b], sorted_rows)

    wait_for(k1, recv.at[0])
    wait_for(v1, recv.at[1])

    def send_kv2(k):
        to = ctx_at(k)
        for n, (source, target) in enumerate(((k1, k2), (v1, v2))):
            away(
                source.at[:, cut(to // QUARTERS, HD)],
                target.at[c],
                send.at[4 + n],
                recv.at[4 + n],
                (to, s),
            ).start()

    each(N_CTX, send_kv2)
    for n, (source, target) in enumerate(((k1, k2), (v1, v2))):
        pltpu.make_async_copy(
            source.at[:, cut(head, HD)], target.at[c], recv.at[4 + n]
        ).start()

    def pass_x(step, carry):
        layer = LAYERS - 1 - step
        wait_for(x1.at[layer], x1_recv.at[layer])

        def send_x2(k):
            to = ctx_at(k)
            away(
                x1.at[layer, cut(to % QUARTERS, ROWS), cut(to // QUARTERS, HD)],
                x2.at[layer, c],
                x2_send.at[layer],
                x2_recv.at[layer],
                (to, s),
            ).start()

        each(N_CTX, send_x2)
        pltpu.make_async_copy(
            x1.at[layer, cut(quarter, ROWS), cut(head, HD)], x2.at[layer, c], x2_recv.at[layer]
        ).start()
        return carry

    lax.fori_loop(0, LAYERS, pass_x, 0)

    wait_for(top2, recv.at[3])
    in_order(top2, g_ref, ROWS, F32)
    dk_ref[...] = jnp.zeros_like(dk_ref)
    dv_ref[...] = jnp.zeros_like(dv_ref)
    for layer in range(LAYERS):
        wait_for(gain1.at[layer], gain_recv.at[layer])
    wait_for(k2, recv.at[4])
    in_order(k2, k_ref, TOK_DEV, BF16)
    for j in range(CHUNKS):
        rows = slice(j * CK, (j + 1) * CK)
        kt_ref[:, rows] = jnp.transpose(k_ref[rows, :])
    wait_for(v2, recv.at[5])
    in_order(v2, v_ref, TOK_DEV, BF16)

    lane = lax.broadcasted_iota(jnp.int32, (1, CQ), 1)
    query_at = (lane // ROWS) * TOK_DEV + quarter * ROWS + lane % ROWS
    key_at = lax.broadcasted_iota(jnp.int32, (CK, CQ), 0)

    def send_g2(layer):
        wait_for(y1.at[layer], g1_recv.at[layer])

        @pl.when(layer != s)
        def _():
            away(
                y1.at[layer],
                grads_out.at[:, cut(s, WIDE)],
                g2_send.at[layer],
                recv.at[6],
                (c, layer),
            ).start()

        @pl.when(layer == s)
        def _():
            pltpu.make_async_copy(y1.at[layer], grads_out.at[:, cut(s, WIDE)], recv.at[6]).start()

    def one_layer(step, carry):
        layer = LAYERS - 1 - step
        wait_for(x2.at[layer], x2_recv.at[layer])
        in_order(x2.at[layer], xw, ROWS, F32)
        xf = xw[...]
        gain = gain1[layer]
        inv_rms = lax.rsqrt(jnp.mean(xf * xf, axis=1, keepdims=True) + norm_eps)
        query = (xf * inv_rms * gain).astype(BF16)
        grad = g_ref[...].astype(BF16)
        seen = key_at <= query_at

        row_max = None
        for j in range(CHUNKS):
            rows, first = slice(j * CK, (j + 1) * CK), j * CQ
            scores = dot(k_ref[rows, :], query[first:, :], NT)
            diag = jnp.where(seen, scores[:, :CQ], masked_score)
            s_ref[rows, first : first + CQ] = diag
            top = jnp.max(diag, axis=0, keepdims=True)
            if j < CHUNKS - 1:
                s_ref[rows, first + CQ :] = scores[:, CQ:]
                rest = jnp.max(scores[:, CQ:], axis=0, keepdims=True)
                top = jnp.concatenate([top, rest], axis=1)
            row_max = max_from(row_max, top, first)

        total = None
        for j in range(CHUNKS):
            rows, first = slice(j * CK, (j + 1) * CK), j * CQ
            e = jnp.exp2((s_ref[rows, first:] - row_max[:, first:]) * (factor * log2e))
            s_ref[rows, first:] = e
            total = add_from(total, jnp.sum(e, axis=0, keepdims=True), first)
        inv_total = 1.0 / total

        delta = None
        for j in range(CHUNKS):
            rows, first = slice(j * CK, (j + 1) * CK), j * CQ
            dp = dot(v_ref[rows, :], grad[first:, :], NT)
            dp_ref[rows, first:] = dp
            probs = s_ref[rows, first:] * inv_total[:, first:]
            s_ref[rows, first:] = probs
            low = probs.astype(BF16)
            part = jnp.sum(low.astype(F32) * dp, axis=0, keepdims=True)
            delta = add_from(delta, part, first)
            dv_ref[rows, :] += dot(low, grad[first:, :], NN)

        dq_t = None
        for j in range(CHUNKS):
            rows, first = slice(j * CK, (j + 1) * CK), j * CQ
            ds = s_ref[rows, first:] * (dp_ref[rows, first:] - delta[:, first:])
            ds = ds.astype(BF16)
            dk_ref[rows, :] += dot(ds, query[first:, :], NN)
            dq_t = add_from(dq_t, dot(kt_ref[:, rows], ds, NN), first)
        scaled = jnp.transpose(dq_t) * (gain * factor)
        inner = jnp.mean(scaled * xf, axis=1, keepdims=True)
        g_ref[...] += inv_rms * scaled - xf * (inv_rms * inv_rms * inv_rms) * inner
        in_blocks(g_ref, ROWS, g1, (layer,))

        def send_g1(k):
            to = ctx_at(k)
            away(
                g1.at[layer, to],
                y1.at[layer, cut(quarter, ROWS), cut(head, HD)],
                g1_send.at[layer],
                g1_recv.at[layer],
                (to, s),
            ).start()

        each(N_CTX, send_g1)
        pltpu.make_async_copy(
            g1.at[layer, c], y1.at[layer, cut(quarter, ROWS), cut(head, HD)], g1_recv.at[layer]
        ).start()

        @pl.when(step >= LAG)
        def _():
            send_g2(layer + LAG)

        return carry

    lax.fori_loop(0, LAYERS, one_layer, 0)

    dk_ref[...] = dk_ref[...] * factor
    in_blocks(dk_ref, TOK_DEV, dk1, ())
    in_blocks(dv_ref, TOK_DEV, dv1, ())

    def send_dkv(k):
        to = ctx_at(k)
        for n, (source, target) in enumerate(((dk1, dk2), (dv1, dv2))):
            away(source.at[to], target.at[c], send.at[7 + n], recv.at[7 + n], (to, s)).start()

    each(N_CTX, send_dkv)
    for n, (source, target) in enumerate(((dk1, dk2), (dv1, dv2))):
        pltpu.make_async_copy(source.at[c], target.at[c], recv.at[7 + n]).start()

    for layer in range(LAG - 1, -1, -1):
        send_g2(layer)

    for n, (part, whole, out) in enumerate(((dk2, dk3, dk_out), (dv2, dv3, dv_out))):
        wait_for(part, recv.at[7 + n])
        for h in range(HEADS_SEC):
            total = part[h * QUARTERS].astype(F32)
            for q in range(1, QUARTERS):
                total = total + part[h * QUARTERS + q].astype(F32)
            whole[:, h * HD : (h + 1) * HD] = total.astype(BF16)

        def send_whole(k):
            to = sec_at(k)
            away(
                whole.at[cut(to, TOK_SEC), :],
                out.at[:, cut(s, WIDE)],
                send.at[9 + n],
                recv.at[9 + n],
                (c, to),
            ).start()

        each(N_SEC, send_whole)
        pltpu.make_async_copy(
            whole.at[cut(s, TOK_SEC), :], out.at[:, cut(s, WIDE)], recv.at[9 + n]
        ).start()

    wait_for(grads_out, recv.at[6])
    wait_for(dk_out, recv.at[9])
    wait_for(dv_out, recv.at[10])
    for n, ref in enumerate((k1, v1)):
        wait_for(ref.at[pl.ds(0, TOK_DEV - TOK_SEC), :], send.at[n])
    wait_for(x1.at[pl.ds(0, N_SEC - 1)], send.at[2])
    wait_for(top2.at[pl.ds(0, N_CTX - 1)], send.at[3])
    for n, ref in enumerate((k2, v2)):
        wait_for(ref.at[pl.ds(0, N_CTX - 1)], send.at[4 + n])
    for n, ref in enumerate((dk2, dv2)):
        wait_for(ref.at[pl.ds(0, N_CTX - 1)], send.at[7 + n])
    for n, ref in enumerate((dk3, dv3)):
        wait_for(ref.at[pl.ds(0, TOK_DEV - TOK_SEC), :], send.at[9 + n])

    def left(layer, carry):
        wait_for(x2.at[layer, pl.ds(0, N_CTX - 1)], x2_send.at[layer])
        wait_for(g1.at[layer, pl.ds(0, N_CTX - 1)], g1_send.at[layer])

        @pl.when(layer != s)
        def _():
            wait_for(y1.at[layer], g2_send.at[layer])

        return carry

    lax.fori_loop(0, LAYERS, left, 0)
    for k in range(1, N_SEC):
        wait_for(gain1.at[0], gain_send.at[k])


def body(x_saved, gains, keys, values, grad_top, block_order):
    smem = pl.BlockSpec(memory_space=pltpu.SMEM)
    anywhere = pl.BlockSpec(memory_space=pl.ANY)
    dma = pltpu.SemaphoreType.DMA
    grads, dk, dv = pl.pallas_call(
        kernel,
        out_shape=(
            jax.ShapeDtypeStruct((TOK_DEV, WIDTH), BF16),
            jax.ShapeDtypeStruct((TOK_SEC, WIDTH), BF16),
            jax.ShapeDtypeStruct((TOK_SEC, WIDTH), BF16),
        ),
        in_specs=[smem] + [anywhere] * 5,
        out_specs=(anywhere,) * 3,
        scratch_shapes=[
            pltpu.VMEM((TOK_DEV, WIDE), BF16),
            pltpu.VMEM((TOK_DEV, WIDE), BF16),
            pltpu.VMEM((LAYERS, TOK_DEV, WIDE), BF16),
            pltpu.VMEM((LAYERS, 1, HD), F32),
            pltpu.VMEM((N_CTX, ROWS, HD), BF16),
            pltpu.VMEM((N_CTX, TOK_DEV, HD), BF16),
            pltpu.VMEM((N_CTX, TOK_DEV, HD), BF16),
            pltpu.VMEM((LAYERS, N_CTX, ROWS, HD), BF16),
            pltpu.VMEM((NQ, HD), F32),
            pltpu.VMEM((NK, HD), BF16),
            pltpu.VMEM((NK, HD), BF16),
            pltpu.VMEM((HD, NK), BF16),
            pltpu.VMEM((NK, NQ), F32),
            pltpu.VMEM((NK, NQ), F32),
            pltpu.VMEM((NQ, HD), F32),
            pltpu.VMEM((NK, HD), F32),
            pltpu.VMEM((NK, HD), F32),
            pltpu.VMEM((LAYERS, N_CTX, ROWS, HD), BF16),
            pltpu.VMEM((LAYERS, TOK_DEV, WIDE), BF16),
            pltpu.VMEM((N_CTX, TOK_DEV, HD), BF16),
            pltpu.VMEM((N_CTX, TOK_DEV, HD), BF16),
            pltpu.VMEM((N_CTX, TOK_DEV, HD), BF16),
            pltpu.VMEM((N_CTX, TOK_DEV, HD), BF16),
            pltpu.VMEM((TOK_DEV, WIDE), BF16),
            pltpu.VMEM((TOK_DEV, WIDE), BF16),
            dma((11,)),
            dma((11,)),
            dma((N_SEC,)),
            dma((N_SEC,)),
            dma((LAYERS,)),
            dma((LAYERS,)),
            dma((LAYERS,)),
            dma((LAYERS,)),
            dma((LAYERS,)),
            dma((LAYERS,)),
        ],
        compiler_params=pltpu.CompilerParams(
            vmem_limit_bytes=56 * 2**20, collective_id=0, has_side_effects=True
        ),
    )(block_order, x_saved, gains, keys, values, grad_top)
    return (grads.astype(F32)[None], dk.astype(F32), dv.astype(F32))


def solution(mesh):
    placed = (
        P("section", "ctx", None),
        P("section", None),
        P(("ctx", "section"), None),
        P(("ctx", "section"), None),
        P("ctx", None),
        P(),
    )
    return jax.shard_map(
        body,
        mesh=mesh,
        in_specs=placed,
        out_specs=(
            P("section", "ctx", None),
            P(("ctx", "section"), None),
            P(("ctx", "section"), None),
        ),
        check_vma=False,
    )
```

```python
import math

import jax
import jax.numpy as jnp
from jax import lax
from jax.experimental import pallas as pl
from jax.experimental.pallas import tpu as pltpu
from jax.sharding import PartitionSpec as P

H = 32
HD = 128
LAYERS = 8
N_SEC = LAYERS
N_CTX = 16
TOK_DEV = 128
WIDTH = H * HD
HEADS_SEC = H // N_SEC
WIDE = HEADS_SEC * HD
N_NEAR = N_CTX // 2
ROWS = TOK_DEV // 2
TOK_SEC = TOK_DEV // N_SEC
NQ = N_NEAR * ROWS
NK = N_CTX * TOK_DEV
PART = 32
PARTS = (0, 2, 1, 3)
CHUNKS = (
    (slice(0, 512), 0),
    (slice(512, 1024), 0),
    (slice(1024, 1280), 0),
    (slice(1280, 1536), 128),
    (slice(1536, 1792), 256),
    (slice(1792, 2048), 384),
)
LAG = 2

masked_score = -1e30
norm_eps = 1e-06
factor = 1.0 / math.sqrt(HD)
log2e = math.log2(math.e)

NT = (((1,), (1,)), ((), ()))
NN = (((1,), (0,)), ((), ()))
BF16, F32 = jnp.bfloat16, jnp.float32


def dot(a, b, dims):
    return lax.dot_general(a, b, dims, preferred_element_type=jnp.float32)


def add_from(total, part, first):
    if total is None:
        return part
    if first == 0:
        return total + part
    return jnp.concatenate([total[:, :first], total[:, first:] + part], axis=1)


def max_from(total, part, first):
    if total is None:
        return part
    if first == 0:
        return jnp.maximum(total, part)
    return jnp.concatenate([total[:, :first], jnp.maximum(total[:, first:], part)], axis=1)


def pick(wanted, options):
    chosen = options[0][1]
    for number, option in options[1:]:
        chosen = lax.select(number == wanted, option, chosen)
    return chosen


def cut(index, size):
    return pl.ds(pl.multiple_of(index * size, size), size)


def kernel(
    place_ref,
    x_hbm,
    gain_hbm,
    keys_hbm,
    values_hbm,
    top_hbm,
    grads_out,
    dk_out,
    dv_out,
    k1,
    v1,
    x1,
    gain1,
    top2,
    k2,
    v2,
    x2,
    xw,
    k_ref,
    v_ref,
    kt_ref,
    bias_ref,
    s_ref,
    dp_ref,
    g_ref,
    dk_ref,
    dv_ref,
    g1,
    y1,
    dk1,
    dv1,
    dk2,
    dv2,
    dk3,
    dv3,
    dk4,
    dv4,
    dk5,
    dv5,
    send,
    recv,
    gain_send,
    gain_recv,
    x1_recv,
    x2_send,
    x2_recv,
    g1_send,
    g1_recv,
    g2_send,
):
    c, s = lax.axis_index("ctx"), lax.axis_index("section")
    y, x_lo, core = c // 4, (c // 2) % 2, c % 2
    other = 1 - core
    mine, near = y * 2 + core, y * 2 + x_lo

    def device(to_y, to_x_lo, to_core):
        return (to_y * 4 + to_x_lo * 2 + to_core, s)

    def sec_at(k):
        return ((s // 2 + k // 2) % 4) * 2 + (s + k) % 2

    def away(source, target, send_sem, recv_sem, to):
        return pltpu.make_async_remote_copy(
            src_ref=source,
            dst_ref=target,
            send_sem=send_sem,
            recv_sem=recv_sem,
            device_id=to,
            device_id_type=pl.DeviceIdType.MESH,
        )

    def wait_for(ref, sem):
        pltpu.make_async_copy(ref, ref, sem).wait()

    def each(first, last, step):
        def run(k, carry):
            step(k)
            return carry

        lax.fori_loop(first, last, run, 0)

    barrier = pltpu.get_barrier_semaphore()

    def greet(to):
        pl.semaphore_signal(barrier, inc=1, device_id=to, device_id_type=pl.DeviceIdType.MESH)

    each(1, N_SEC, lambda k: greet((c, sec_at(k))))
    each(1, 4, lambda k: greet(device((y + k) % 4, x_lo, core)))
    each(0, 4, lambda k: greet(device((y + k) % 4, x_lo, other)))
    each(0, 4, lambda k: greet(device((y + k) % 4, 1 - x_lo, core)))
    pl.semaphore_wait(barrier, N_SEC - 1 + 11)

    first_hop = ((keys_hbm, k1), (values_hbm, v1))

    def send_kv1(k):
        to = sec_at(k)
        for n, (source, target) in enumerate(first_hop):
            away(
                source.at[:, cut(to, WIDE)],
                target.at[cut(s, TOK_SEC), :],
                send.at[n],
                recv.at[n],
                (c, to),
            ).start()

    each(1, N_SEC, send_kv1)
    for n, (source, target) in enumerate(first_hop):
        pltpu.make_async_copy(
            source.at[:, cut(s, WIDE)], target.at[cut(s, TOK_SEC), :], recv.at[n]
        ).start()

    def send_gain(k):
        to = sec_at(k)
        away(
            gain_hbm.at[:, cut(to * HEADS_SEC + y, HD)],
            gain1.at[s],
            gain_send.at[k],
            gain_recv.at[s],
            (c, to),
        ).start()

    each(1, N_SEC, send_gain)
    pltpu.make_async_copy(
        gain_hbm.at[:, cut(s * HEADS_SEC + y, HD)], gain1.at[s], gain_recv.at[s]
    ).start()

    for part in PARTS:
        rows = pl.ds(part * PART, PART)

        def send_x1(k):
            to = sec_at(k)
            away(
                x_hbm.at[0, rows, cut(to, WIDE)],
                x1.at[s, rows, :],
                send.at[2],
                x1_recv.at[s, part],
                (c, to),
            ).start()

        each(1, N_SEC, send_x1)
        pltpu.make_async_copy(
            x_hbm.at[0, rows, cut(s, WIDE)], x1.at[s, rows, :], x1_recv.at[s, part]
        ).start()

    def send_top(to_y, to_core):
        away(
            top_hbm.at[cut(to_core, ROWS), cut(s * HEADS_SEC + to_y, HD)],
            top2.at[mine],
            send.at[3],
            recv.at[3],
            device(to_y, x_lo, to_core),
        ).start()

    each(1, 4, lambda k: send_top((y + k) % 4, core))
    each(0, 4, lambda k: send_top((y + k) % 4, other))
    pltpu.make_async_copy(
        top_hbm.at[cut(core, ROWS), cut(s * HEADS_SEC + y, HD)], top2.at[mine], recv.at[3]
    ).start()

    places = [place_ref[b] for b in range(N_CTX)]
    near_places = [place_ref[(e // 2) * 4 + x_lo * 2 + e % 2] for e in range(N_NEAR)]
    ranks = []
    for e in range(N_NEAR):
        rank = 0
        for f in range(N_NEAR):
            if f != e:
                rank = rank + jnp.where(near_places[f] < near_places[e], 1, 0)
        ranks.append(rank)

    def in_order(ref, numbers, target, size, kind):
        blocks = [(number, ref[n]) for n, number in enumerate(numbers)]
        for p in range(len(numbers)):
            target[p * size : (p + 1) * size, :] = pick(p, blocks).astype(kind)

    lane = lax.broadcasted_iota(jnp.int32, (1, NQ), 1)
    query_at = core * ROWS + lane % ROWS
    for e in range(N_NEAR):
        query_at = query_at + jnp.where(lane // ROWS == ranks[e], near_places[e] * TOK_DEV, 0)

    def make_bias(n, carry):
        key_at = lax.broadcasted_iota(jnp.int32, (TOK_DEV, NQ), 0) + n * TOK_DEV
        bias_ref[cut(n, TOK_DEV), :] = jnp.where(key_at <= query_at, 0.0, masked_score)
        return carry

    second_hop = ((k1, k2), (v1, v2))
    wait_for(k1, recv.at[0])
    wait_for(v1, recv.at[1])

    def send_kv2(to_y, to_x_lo):
        for n, (source, target) in enumerate(second_hop):
            away(
                source.at[:, cut(to_y, HD)],
                target.at[core, near],
                send.at[4 + n],
                recv.at[4 + n],
                device(to_y, to_x_lo, core),
            ).start()

    each(0, 4, lambda k: send_kv2((y + k) % 4, 1 - x_lo))
    each(1, 4, lambda k: send_kv2((y + k) % 4, x_lo))
    for n, (source, target) in enumerate(second_hop):
        pltpu.make_async_copy(
            source.at[:, cut(y, HD)], target.at[core, near], recv.at[4 + n]
        ).start()

    def pass_x(part):
        to_core = part // (ROWS // PART)
        rows = pl.ds(part * PART, PART)
        at = pl.ds(part % (ROWS // PART) * PART, PART)

        def one(step, carry):
            layer = LAYERS - 1 - step
            wait_for(x1.at[layer, rows, :], x1_recv.at[layer, part])

            def send_x2(to_y):
                away(
                    x1.at[layer, rows, cut(to_y, HD)],
                    x2.at[layer, mine, at, :],
                    x2_send.at[layer],
                    x2_recv.at[layer],
                    device(to_y, x_lo, to_core),
                ).start()

            each(1, 4, lambda k: send_x2((y + k) % 4))

            @pl.when(core != to_core)
            def _():
                send_x2(y)

            @pl.when(core == to_core)
            def _():
                pltpu.make_async_copy(
                    x1.at[layer, rows, cut(y, HD)], x2.at[layer, mine, at, :], x2_recv.at[layer]
                ).start()

            return carry

        lax.fori_loop(0, LAYERS, one, 0)

    for part in PARTS[:2]:
        pass_x(part)

    for n, ref in enumerate((k2, v2)):
        wait_for(ref.at[core], recv.at[4 + n])
        away(
            ref.at[core], ref.at[core], send.at[6 + n], recv.at[6 + n], device(y, x_lo, other)
        ).start()
    lax.fori_loop(0, N_CTX, make_bias, 0)
    for part in PARTS[2:]:
        pass_x(part)

    wait_for(top2, recv.at[3])
    in_order(top2, ranks, g_ref, ROWS, F32)
    dk_ref[...] = jnp.zeros_like(dk_ref)
    dv_ref[...] = jnp.zeros_like(dv_ref)
    for layer in range(LAYERS):
        wait_for(gain1.at[layer], gain_recv.at[layer])

    wait_for(k2.at[other], recv.at[6])
    wait_for(v2.at[other], recv.at[7])
    for ref, target in ((k2, k_ref), (v2, v_ref)):
        blocks = [(places[b], ref[b % 2, b // 2]) for b in range(N_CTX)]
        for p in range(N_CTX):
            target[p * TOK_DEV : (p + 1) * TOK_DEV, :] = pick(p, blocks)
    for n in range(4):
        rows = slice(n * 512, (n + 1) * 512)
        kt_ref[:, rows] = jnp.transpose(k_ref[rows, :])

    def send_g2(layer):
        wait_for(y1.at[layer], g1_recv.at[layer])

        @pl.when(layer != s)
        def _():
            away(
                y1.at[layer],
                grads_out.at[:, cut(s, WIDE)],
                g2_send.at[layer],
                recv.at[8],
                (c, layer),
            ).start()

        @pl.when(layer == s)
        def _():
            pltpu.make_async_copy(y1.at[layer], grads_out.at[:, cut(s, WIDE)], recv.at[8]).start()

    def one_layer(step, carry):
        layer = LAYERS - 1 - step
        wait_for(x2.at[layer], x2_recv.at[layer])
        in_order(x2.at[layer], ranks, xw, ROWS, F32)
        xf = xw[...]
        gain = gain1[layer]
        inv_rms = lax.rsqrt(jnp.mean(xf * xf, axis=1, keepdims=True) + norm_eps)
        query = (xf * inv_rms * gain).astype(BF16)
        grad = g_ref[...].astype(BF16)

        row_max = None
        for rows, first in CHUNKS:
            scores = dot(k_ref[rows, :], query[first:, :], NT) + bias_ref[rows, first:]
            s_ref[rows, first:] = scores
            row_max = max_from(row_max, jnp.max(scores, axis=0, keepdims=True), first)

        total = None
        for rows, first in CHUNKS:
            e = jnp.exp2((s_ref[rows, first:] - row_max[:, first:]) * (factor * log2e))
            s_ref[rows, first:] = e
            total = add_from(total, jnp.sum(e, axis=0, keepdims=True), first)
        inv_total = 1.0 / total

        delta = None
        for rows, first in CHUNKS:
            dp = dot(v_ref[rows, :], grad[first:, :], NT)
            dp_ref[rows, first:] = dp
            probs = s_ref[rows, first:] * inv_total[:, first:]
            s_ref[rows, first:] = probs
            low = probs.astype(BF16)
            part = jnp.sum(low.astype(F32) * dp, axis=0, keepdims=True)
            delta = add_from(delta, part, first)
            dv_ref[rows, :] += dot(low, grad[first:, :], NN)

        dq_t = None
        for rows, first in CHUNKS:
            ds = s_ref[rows, first:] * (dp_ref[rows, first:] - delta[:, first:])
            ds = ds.astype(BF16)
            dk_ref[rows, :] += dot(ds, query[first:, :], NN)
            dq_t = add_from(dq_t, dot(kt_ref[:, rows], ds, NN), first)
        scaled = jnp.transpose(dq_t) * (gain * factor)
        inner = jnp.mean(scaled * xf, axis=1, keepdims=True)
        g_ref[...] += inv_rms * scaled - xf * (inv_rms * inv_rms * inv_rms) * inner
        by_rank = [(r, g_ref[r * ROWS : (r + 1) * ROWS, :].astype(BF16)) for r in range(N_NEAR)]
        for e in range(N_NEAR):
            g1[layer, e] = pick(ranks[e], by_rank)

        def send_g1(to_y, to_core):
            away(
                g1.at[layer, to_y * 2 + to_core],
                y1.at[layer, cut(core, ROWS), cut(y, HD)],
                g1_send.at[layer],
                g1_recv.at[layer],
                device(to_y, x_lo, to_core),
            ).start()

        each(1, 4, lambda k: send_g1((y + k) % 4, core))
        each(0, 4, lambda k: send_g1((y + k) % 4, other))
        pltpu.make_async_copy(
            g1.at[layer, mine], y1.at[layer, cut(core, ROWS), cut(y, HD)], g1_recv.at[layer]
        ).start()

        @pl.when(step >= LAG)
        def _():
            send_g2(layer + LAG)

        return carry

    lax.fori_loop(0, LAYERS, one_layer, 0)

    dk_ref[...] = dk_ref[...] * factor
    sums = (
        (dk_ref, dk1, dk2, dk3, dk4, dk5, dk_out),
        (dv_ref, dv1, dv2, dv3, dv4, dv5, dv_out),
    )

    def in_blocks(ref, of_core, kind):
        by_place = [
            (p, ref[p * TOK_DEV : (p + 1) * TOK_DEV, :].astype(kind)) for p in range(N_CTX)
        ]
        for f in range(N_NEAR):
            yield f, pick(place_ref[f * 2 + of_core], by_place)

    for n, (ref, part1, part2, _, _, _, _) in enumerate(sums):
        for f, rows in in_blocks(ref, other, BF16):
            part1[f] = rows
        away(part1, part2, send.at[8 + n], recv.at[9 + n], device(y, x_lo, other)).start()

    for n, (ref, _, part2, part3, part4, _, _) in enumerate(sums):
        wait_for(part2, recv.at[9 + n])
        for f, rows in in_blocks(ref, core, F32):
            part3[f] = (rows + part2[f].astype(F32)).astype(BF16)

        def send_sum(to_y, to_x_lo):
            away(
                part3.at[to_y * 2 + to_x_lo],
                part4.at[near],
                send.at[10 + n],
                recv.at[11 + n],
                device(to_y, to_x_lo, core),
            ).start()

        each(0, 4, lambda k: send_sum((y + k) % 4, 1 - x_lo))
        each(1, 4, lambda k: send_sum((y + k) % 4, x_lo))
        pltpu.make_async_copy(part3.at[near], part4.at[near], recv.at[11 + n]).start()

    for layer in range(LAG - 1, -1, -1):
        send_g2(layer)

    for n, (_, _, _, _, part4, part5, out) in enumerate(sums):
        wait_for(part4, recv.at[11 + n])
        for h in range(HEADS_SEC):
            both = part4[h * 2].astype(F32) + part4[h * 2 + 1].astype(F32)
            part5[:, h * HD : (h + 1) * HD] = both.astype(BF16)

        def send_whole(k):
            to = sec_at(k)
            away(
                part5.at[cut(to, TOK_SEC), :],
                out.at[:, cut(s, WIDE)],
                send.at[12 + n],
                recv.at[13 + n],
                (c, to),
            ).start()

        each(1, N_SEC, send_whole)
        pltpu.make_async_copy(
            part5.at[cut(s, TOK_SEC), :], out.at[:, cut(s, WIDE)], recv.at[13 + n]
        ).start()

    wait_for(grads_out, recv.at[8])
    wait_for(dk_out, recv.at[13])
    wait_for(dv_out, recv.at[14])
    most = pl.ds(0, N_SEC - 1)
    for n, ref in enumerate((k1, v1)):
        wait_for(ref.at[pl.ds(0, TOK_DEV - TOK_SEC), :], send.at[n])
    wait_for(x1.at[most], send.at[2])
    wait_for(top2.at[most], send.at[3])
    for n, ref in enumerate((k2, v2)):
        wait_for(ref.at[0, most], send.at[4 + n])
        wait_for(ref.at[0], send.at[6 + n])
    for n, (_, part1, _, part3, _, part5, _) in enumerate(sums):
        wait_for(part1, send.at[8 + n])
        wait_for(part3.at[most], send.at[10 + n])
        wait_for(part5.at[pl.ds(0, TOK_DEV - TOK_SEC), :], send.at[12 + n])

    def left(layer, carry):
        wait_for(x2.at[layer, most], x2_send.at[layer])
        wait_for(g1.at[layer, most], g1_send.at[layer])

        @pl.when(layer != s)
        def _():
            wait_for(y1.at[layer], g2_send.at[layer])

        return carry

    lax.fori_loop(0, LAYERS, left, 0)
    for k in range(1, N_SEC):
        wait_for(gain1.at[0], gain_send.at[k])


def body(x_saved, gains, keys, values, grad_top, block_order):
    smem = pl.BlockSpec(memory_space=pltpu.SMEM)
    anywhere = pl.BlockSpec(memory_space=pl.ANY)
    dma = pltpu.SemaphoreType.DMA
    grads, dk, dv = pl.pallas_call(
        kernel,
        out_shape=(
            jax.ShapeDtypeStruct((TOK_DEV, WIDTH), BF16),
            jax.ShapeDtypeStruct((TOK_SEC, WIDTH), BF16),
            jax.ShapeDtypeStruct((TOK_SEC, WIDTH), BF16),
        ),
        in_specs=[smem] + [anywhere] * 5,
        out_specs=(anywhere,) * 3,
        scratch_shapes=[
            pltpu.VMEM((TOK_DEV, WIDE), BF16),
            pltpu.VMEM((TOK_DEV, WIDE), BF16),
            pltpu.VMEM((LAYERS, TOK_DEV, WIDE), BF16),
            pltpu.VMEM((LAYERS, 1, HD), F32),
            pltpu.VMEM((N_NEAR, ROWS, HD), BF16),
            pltpu.VMEM((2, N_NEAR, TOK_DEV, HD), BF16),
            pltpu.VMEM((2, N_NEAR, TOK_DEV, HD), BF16),
            pltpu.VMEM((LAYERS, N_NEAR, ROWS, HD), BF16),
            pltpu.VMEM((NQ, HD), F32),
            pltpu.VMEM((NK, HD), BF16),
            pltpu.VMEM((NK, HD), BF16),
            pltpu.VMEM((HD, NK), BF16),
            pltpu.VMEM((NK, NQ), F32),
            pltpu.VMEM((NK, NQ), F32),
            pltpu.VMEM((NK, NQ), F32),
            pltpu.VMEM((NQ, HD), F32),
            pltpu.VMEM((NK, HD), F32),
            pltpu.VMEM((NK, HD), F32),
            pltpu.VMEM((LAYERS, N_NEAR, ROWS, HD), BF16),
            pltpu.VMEM((LAYERS, TOK_DEV, WIDE), BF16),
        ]
        + [pltpu.VMEM((N_NEAR, TOK_DEV, HD), BF16)] * 8
        + [pltpu.VMEM((TOK_DEV, WIDE), BF16)] * 2
        + [
            dma((14,)),
            dma((15,)),
            dma((N_SEC,)),
            dma((N_SEC,)),
            dma((LAYERS, TOK_DEV // PART)),
            dma((LAYERS,)),
            dma((LAYERS,)),
            dma((LAYERS,)),
            dma((LAYERS,)),
            dma((LAYERS,)),
        ],
        compiler_params=pltpu.CompilerParams(
            vmem_limit_bytes=56 * 2**20, collective_id=0, has_side_effects=True
        ),
    )(block_order, x_saved, gains, keys, values, grad_top)
    return (grads.astype(F32)[None], dk.astype(F32), dv.astype(F32))


def solution(mesh):
    placed = (
        P("section", "ctx", None),
        P("section", None),
        P(("ctx", "section"), None),
        P(("ctx", "section"), None),
        P("ctx", None),
        P(),
    )
    return jax.shard_map(
        body,
        mesh=mesh,
        in_specs=placed,
        out_specs=(
            P("section", "ctx", None),
            P(("ctx", "section"), None),
            P(("ctx", "section"), None),
        ),
        check_vma=False,
    )
```

```python
import math

import jax
import jax.numpy as jnp
from jax import lax
from jax.experimental import pallas as pl
from jax.experimental.pallas import tpu as pltpu
from jax.sharding import PartitionSpec as P

H = 32
HD = 128
LAYERS = 8
N_SEC = LAYERS
N_CTX = 16
TOK_DEV = 128
WIDTH = H * HD
HEADS_SEC = H // N_SEC
WIDE = HEADS_SEC * HD
N_NEAR = N_CTX // 2
ROWS = TOK_DEV // 2
TOK_SEC = TOK_DEV // N_SEC
NQ = N_NEAR * ROWS
NK = N_CTX * TOK_DEV
PART = ROWS // 2
CHUNKS = (
    (slice(0, 512), 0),
    (slice(512, 1024), 0),
    (slice(1024, 1280), 0),
    (slice(1280, 1536), 128),
    (slice(1536, 1792), 256),
    (slice(1792, 2048), 384),
)
LAG = 2
WIDEN_STEPS = 4

masked_score = -1e30
norm_eps = 1e-06
factor = 1.0 / math.sqrt(HD)
log2e = math.log2(math.e)

NT = (((1,), (1,)), ((), ()))
NN = (((1,), (0,)), ((), ()))
BF16, F32 = jnp.bfloat16, jnp.float32


def dot(a, b, dims):
    return lax.dot_general(a, b, dims, preferred_element_type=jnp.float32)


def add_from(total, part, first):
    if total is None:
        return part
    if first == 0:
        return total + part
    return jnp.concatenate([total[:, :first], total[:, first:] + part], axis=1)


def max_from(total, part, first):
    if total is None:
        return part
    if first == 0:
        return jnp.maximum(total, part)
    return jnp.concatenate([total[:, :first], jnp.maximum(total[:, first:], part)], axis=1)


def pick(wanted, options):
    chosen = options[0][1]
    for number, option in options[1:]:
        chosen = lax.select(number == wanted, option, chosen)
    return chosen


def cut(index, size):
    return pl.ds(pl.multiple_of(index * size, size), size)


def kernel(
    place_ref,
    x_hbm,
    gain_hbm,
    keys_hbm,
    values_hbm,
    top_hbm,
    grads_out,
    dk_out,
    dv_out,
    k1,
    v1,
    x1,
    z1,
    gain1,
    top2,
    k2,
    v2,
    x2,
    xw,
    k_ref,
    v_ref,
    kt_ref,
    bias_ref,
    s_ref,
    dp_ref,
    g_ref,
    dk_ref,
    dv_ref,
    g1,
    y1,
    dk1,
    dv1,
    dk2,
    dv2,
    dk3,
    dv3,
    dk4,
    dv4,
    dk5,
    dv5,
    send,
    recv,
    gain_send,
    gain_recv,
    x1_recv,
    x2_send,
    x2_recv,
    z1_recv,
    z2_recv,
    g1_send,
    g1_recv,
    g2_send,
):
    c, s = lax.axis_index("ctx"), lax.axis_index("section")
    y, x_lo, core = c // 4, (c // 2) % 2, c % 2
    other = 1 - core
    mine, near = y * 2 + core, y * 2 + x_lo

    def device(to_y, to_x_lo, to_core):
        return (to_y * 4 + to_x_lo * 2 + to_core, s)

    def sec_at(k):
        return ((s // 2 + k // 2) % 4) * 2 + (s + k) % 2

    def away(source, target, send_sem, recv_sem, to):
        return pltpu.make_async_remote_copy(
            src_ref=source,
            dst_ref=target,
            send_sem=send_sem,
            recv_sem=recv_sem,
            device_id=to,
            device_id_type=pl.DeviceIdType.MESH,
        )

    def wait_for(ref, sem):
        pltpu.make_async_copy(ref, ref, sem).wait()

    def each(first, last, step):
        def run(k, carry):
            step(k)
            return carry

        lax.fori_loop(first, last, run, 0)

    barrier = pltpu.get_barrier_semaphore()

    def greet(to):
        pl.semaphore_signal(barrier, inc=1, device_id=to, device_id_type=pl.DeviceIdType.MESH)

    each(1, N_SEC, lambda k: greet((c, sec_at(k))))
    each(1, 4, lambda k: greet(device((y + k) % 4, x_lo, core)))
    each(0, 4, lambda k: greet(device((y + k) % 4, x_lo, other)))
    each(0, 4, lambda k: greet(device((y + k) % 4, 1 - x_lo, core)))
    pl.semaphore_wait(barrier, N_SEC - 1 + 11)

    first_hop = ((keys_hbm, k1), (values_hbm, v1))

    def send_kv1(k):
        to = sec_at(k)
        for n, (source, target) in enumerate(first_hop):
            away(
                source.at[:, cut(to, WIDE)],
                target.at[cut(s, TOK_SEC), :],
                send.at[n],
                recv.at[n],
                (c, to),
            ).start()

    each(1, N_SEC, send_kv1)
    for n, (source, target) in enumerate(first_hop):
        pltpu.make_async_copy(
            source.at[:, cut(s, WIDE)], target.at[cut(s, TOK_SEC), :], recv.at[n]
        ).start()

    def send_gain(k):
        to = sec_at(k)
        away(
            gain_hbm.at[:, cut(to * HEADS_SEC + y, HD)],
            gain1.at[s],
            gain_send.at[k],
            gain_recv.at[s],
            (c, to),
        ).start()

    each(1, N_SEC, send_gain)
    pltpu.make_async_copy(
        gain_hbm.at[:, cut(s * HEADS_SEC + y, HD)], gain1.at[s], gain_recv.at[s]
    ).start()

    for to_core in range(2):
        rows = pl.ds(to_core * ROWS, PART)

        def send_x1(k):
            to = sec_at(k)
            away(
                x_hbm.at[0, rows, cut(to, WIDE)],
                x1.at[s, to_core],
                send.at[2],
                x1_recv.at[s, to_core],
                (c, to),
            ).start()

        each(1, N_SEC, send_x1)
        pltpu.make_async_copy(
            x_hbm.at[0, rows, cut(s, WIDE)], x1.at[s, to_core], x1_recv.at[s, to_core]
        ).start()

    def send_z1(k):
        to_sec = sec_at(k)

        def rows_for(to_y, to_core):
            return x_hbm.at[
                0, pl.ds(to_core * ROWS + PART, PART), cut(to_sec * HEADS_SEC + to_y, HD)
            ]

        def send_to(to_y, to_core):
            away(
                rows_for(to_y, to_core),
                z1.at[to_sec, mine],
                send.at[14],
                z1_recv.at[to_sec],
                device(to_y, x_lo, to_core),
            ).start()

        each(1, 4, lambda q: send_to((y + q) % 4, core))
        each(0, 4, lambda q: send_to((y + q) % 4, other))
        pltpu.make_async_copy(
            rows_for(y, core), z1.at[to_sec, mine], z1_recv.at[to_sec]
        ).start()

    each(1, N_SEC + 1, send_z1)

    def send_top(to_y, to_core):
        away(
            top_hbm.at[cut(to_core, ROWS), cut(s * HEADS_SEC + to_y, HD)],
            top2.at[mine],
            send.at[3],
            recv.at[3],
            device(to_y, x_lo, to_core),
        ).start()

    each(1, 4, lambda k: send_top((y + k) % 4, core))
    each(0, 4, lambda k: send_top((y + k) % 4, other))
    pltpu.make_async_copy(
        top_hbm.at[cut(core, ROWS), cut(s * HEADS_SEC + y, HD)], top2.at[mine], recv.at[3]
    ).start()

    places = [place_ref[b] for b in range(N_CTX)]
    near_places = [place_ref[(e // 2) * 4 + x_lo * 2 + e % 2] for e in range(N_NEAR)]
    ranks = []
    for e in range(N_NEAR):
        rank = 0
        for f in range(N_NEAR):
            if f != e:
                rank = rank + jnp.where(near_places[f] < near_places[e], 1, 0)
        ranks.append(rank)

    def in_order(ref, numbers, target, size, kind):
        blocks = [(number, ref[n]) for n, number in enumerate(numbers)]
        for p in range(len(numbers)):
            target[p * size : (p + 1) * size, :] = pick(p, blocks).astype(kind)

    lane = lax.broadcasted_iota(jnp.int32, (1, NQ), 1)
    query_at = core * ROWS + lane % ROWS
    for e in range(N_NEAR):
        query_at = query_at + jnp.where(lane // ROWS == ranks[e], near_places[e] * TOK_DEV, 0)

    def make_bias(n, carry):
        key_at = lax.broadcasted_iota(jnp.int32, (TOK_DEV, NQ), 0) + n * TOK_DEV
        bias_ref[cut(n, TOK_DEV), :] = jnp.where(key_at <= query_at, 0.0, masked_score)
        return carry

    second_hop = ((k1, k2), (v1, v2))
    wait_for(k1, recv.at[0])
    wait_for(v1, recv.at[1])

    def send_kv2(to_y, to_x_lo):
        for n, (source, target) in enumerate(second_hop):
            away(
                source.at[:, cut(to_y, HD)],
                target.at[core, near],
                send.at[4 + n],
                recv.at[4 + n],
                device(to_y, to_x_lo, core),
            ).start()

    each(0, 4, lambda k: send_kv2((y + k) % 4, 1 - x_lo))
    each(1, 4, lambda k: send_kv2((y + k) % 4, x_lo))
    for n, (source, target) in enumerate(second_hop):
        pltpu.make_async_copy(
            source.at[:, cut(y, HD)], target.at[core, near], recv.at[4 + n]
        ).start()

    def pass_z(k):
        to = sec_at(k)
        wait_for(z1.at[to], z1_recv.at[to])
        target = x2.at[s, :, pl.ds(PART, PART), :]

        @pl.when(to != s)
        def _():
            away(z1.at[to], target, send.at[15], z2_recv.at[s], (c, to)).start()

        @pl.when(to == s)
        def _():
            pltpu.make_async_copy(z1.at[to], target, z2_recv.at[s]).start()

    def pass_x(to_core):
        def one(step, carry):
            layer = LAYERS - 1 - step
            wait_for(x1.at[layer, to_core], x1_recv.at[layer, to_core])
            target = x2.at[layer, mine, pl.ds(0, PART), :]

            def send_x2(to_y):
                away(
                    x1.at[layer, to_core, :, cut(to_y, HD)],
                    target,
                    x2_send.at[layer],
                    x2_recv.at[layer],
                    device(to_y, x_lo, to_core),
                ).start()

            each(1, 4, lambda k: send_x2((y + k) % 4))

            @pl.when(core != to_core)
            def _():
                send_x2(y)

            @pl.when(core == to_core)
            def _():
                pltpu.make_async_copy(
                    x1.at[layer, to_core, :, cut(y, HD)], target, x2_recv.at[layer]
                ).start()

            return carry

        lax.fori_loop(0, LAYERS, one, 0)

    pass_x(0)
    each(1, N_SEC + 1, pass_z)
    pass_x(1)

    for n, ref in enumerate((k2, v2)):
        wait_for(ref.at[core], recv.at[4 + n])
        away(
            ref.at[core], ref.at[core], send.at[6 + n], recv.at[6 + n], device(y, x_lo, other)
        ).start()
    lax.fori_loop(0, N_CTX, make_bias, 0)
    wait_for(top2, recv.at[3])
    in_order(top2, ranks, g_ref, ROWS, F32)
    dk_ref[...] = jnp.zeros_like(dk_ref)
    dv_ref[...] = jnp.zeros_like(dv_ref)
    for layer in range(LAYERS):
        wait_for(gain1.at[layer], gain_recv.at[layer])

    wait_for(k2.at[other], recv.at[6])
    wait_for(v2.at[other], recv.at[7])
    for ref, target in ((k2, k_ref), (v2, v_ref)):
        blocks = [(places[b], ref[b % 2, b // 2]) for b in range(N_CTX)]
        for p in range(N_CTX):
            target[p * TOK_DEV : (p + 1) * TOK_DEV, :] = pick(p, blocks)
    for n in range(4):
        rows = slice(n * 512, (n + 1) * 512)
        kt_ref[:, rows] = jnp.transpose(k_ref[rows, :])

    def send_g2(layer):
        wait_for(y1.at[layer], g1_recv.at[layer])

        @pl.when(layer != s)
        def _():
            away(
                y1.at[layer],
                grads_out.at[:, cut(s, WIDE)],
                g2_send.at[layer],
                recv.at[8],
                (c, layer),
            ).start()

        @pl.when(layer == s)
        def _():
            pltpu.make_async_copy(y1.at[layer], grads_out.at[:, cut(s, WIDE)], recv.at[8]).start()

    def one_layer(step, carry):
        layer = LAYERS - 1 - step
        wait_for(x2.at[layer, :, pl.ds(0, PART), :], x2_recv.at[layer])
        wait_for(x2.at[layer, :, pl.ds(PART, PART), :], z2_recv.at[layer])
        in_order(x2.at[layer], ranks, xw, ROWS, F32)
        xf = xw[...]
        gain = gain1[layer]
        inv_rms = lax.rsqrt(jnp.mean(xf * xf, axis=1, keepdims=True) + norm_eps)
        query = (xf * inv_rms * gain).astype(BF16)
        grad = g_ref[...].astype(BF16)

        row_max = None
        for rows, first in CHUNKS:
            scores = dot(k_ref[rows, :], query[first:, :], NT) + bias_ref[rows, first:]
            s_ref[rows, first:] = scores
            row_max = max_from(row_max, jnp.max(scores, axis=0, keepdims=True), first)

        total = None
        for rows, first in CHUNKS:
            e = jnp.exp2((s_ref[rows, first:] - row_max[:, first:]) * (factor * log2e))
            s_ref[rows, first:] = e
            total = add_from(total, jnp.sum(e, axis=0, keepdims=True), first)
        inv_total = 1.0 / total

        delta = None
        for rows, first in CHUNKS:
            dp = dot(v_ref[rows, :], grad[first:, :], NT)
            dp_ref[rows, first:] = dp
            probs = s_ref[rows, first:] * inv_total[:, first:]
            s_ref[rows, first:] = probs
            low = probs.astype(BF16)
            part = jnp.sum(low.astype(F32) * dp, axis=0, keepdims=True)
            delta = add_from(delta, part, first)
            dv_ref[rows, :] += dot(low, grad[first:, :], NN)

        dq_t = None
        for rows, first in CHUNKS:
            ds = s_ref[rows, first:] * (dp_ref[rows, first:] - delta[:, first:])
            ds = ds.astype(BF16)
            dk_ref[rows, :] += dot(ds, query[first:, :], NN)
            dq_t = add_from(dq_t, dot(kt_ref[:, rows], ds, NN), first)
        scaled = jnp.transpose(dq_t) * (gain * factor)
        inner = jnp.mean(scaled * xf, axis=1, keepdims=True)
        g_ref[...] += inv_rms * scaled - xf * (inv_rms * inv_rms * inv_rms) * inner
        by_rank = [(r, g_ref[r * ROWS : (r + 1) * ROWS, :].astype(BF16)) for r in range(N_NEAR)]
        for e in range(N_NEAR):
            g1[layer, e] = pick(ranks[e], by_rank)

        def send_g1(to_y, to_core):
            away(
                g1.at[layer, to_y * 2 + to_core],
                y1.at[layer, cut(core, ROWS), cut(y, HD)],
                g1_send.at[layer],
                g1_recv.at[layer],
                device(to_y, x_lo, to_core),
            ).start()

        each(1, 4, lambda k: send_g1((y + k) % 4, core))
        each(0, 4, lambda k: send_g1((y + k) % 4, other))
        pltpu.make_async_copy(
            g1.at[layer, mine], y1.at[layer, cut(core, ROWS), cut(y, HD)], g1_recv.at[layer]
        ).start()

        @pl.when(step >= LAG)
        def _():
            send_g2(layer + LAG)

        return carry

    lax.fori_loop(0, LAYERS, one_layer, 0)

    dk_ref[...] = dk_ref[...] * factor
    sums = (
        (dk_ref, dk1, dk2, dk3, dk4, dk5, dk_out),
        (dv_ref, dv1, dv2, dv3, dv4, dv5, dv_out),
    )

    def in_blocks(ref, of_core, kind):
        by_place = [
            (p, ref[p * TOK_DEV : (p + 1) * TOK_DEV, :].astype(kind)) for p in range(N_CTX)
        ]
        for f in range(N_NEAR):
            yield f, pick(place_ref[f * 2 + of_core], by_place)

    for n, (ref, part1, part2, _, _, _, _) in enumerate(sums):
        for f, rows in in_blocks(ref, other, BF16):
            part1[f] = rows
        away(part1, part2, send.at[8 + n], recv.at[9 + n], device(y, x_lo, other)).start()

    for n, (ref, _, part2, part3, part4, _, _) in enumerate(sums):
        wait_for(part2, recv.at[9 + n])
        for f, rows in in_blocks(ref, core, F32):
            part3[f] = (rows + part2[f].astype(F32)).astype(BF16)

        def send_sum(to_y, to_x_lo):
            away(
                part3.at[to_y * 2 + to_x_lo],
                part4.at[near],
                send.at[10 + n],
                recv.at[11 + n],
                device(to_y, to_x_lo, core),
            ).start()

        each(0, 4, lambda k: send_sum((y + k) % 4, 1 - x_lo))
        each(1, 4, lambda k: send_sum((y + k) % 4, x_lo))
        pltpu.make_async_copy(part3.at[near], part4.at[near], recv.at[11 + n]).start()

    for layer in range(LAG - 1, -1, -1):
        send_g2(layer)

    for n, (_, _, _, _, part4, part5, out) in enumerate(sums):
        wait_for(part4, recv.at[11 + n])
        for h in range(HEADS_SEC):
            both = part4[h * 2].astype(F32) + part4[h * 2 + 1].astype(F32)
            part5[:, h * HD : (h + 1) * HD] = both.astype(BF16)

        def send_whole(k):
            to = sec_at(k)
            away(
                part5.at[cut(to, TOK_SEC), :],
                out.at[:, cut(s, WIDE)],
                send.at[12 + n],
                recv.at[13 + n],
                (c, to),
            ).start()

        each(1, N_SEC, send_whole)
        pltpu.make_async_copy(
            part5.at[cut(s, TOK_SEC), :], out.at[:, cut(s, WIDE)], recv.at[13 + n]
        ).start()

    wait_for(grads_out, recv.at[8])
    wait_for(dk_out, recv.at[13])
    wait_for(dv_out, recv.at[14])
    most = pl.ds(0, N_SEC - 1)
    for n, ref in enumerate((k1, v1)):
        wait_for(ref.at[pl.ds(0, TOK_DEV - TOK_SEC), :], send.at[n])
    wait_for(x1.at[most], send.at[2])
    wait_for(z1.at[:, most], send.at[14])
    wait_for(z1.at[most], send.at[15])
    wait_for(top2.at[most], send.at[3])
    for n, ref in enumerate((k2, v2)):
        wait_for(ref.at[0, most], send.at[4 + n])
        wait_for(ref.at[0], send.at[6 + n])
    for n, (_, part1, _, part3, _, part5, _) in enumerate(sums):
        wait_for(part1, send.at[8 + n])
        wait_for(part3.at[most], send.at[10 + n])
        wait_for(part5.at[pl.ds(0, TOK_DEV - TOK_SEC), :], send.at[12 + n])

    def left(layer, carry):
        wait_for(x2.at[layer, most, pl.ds(0, PART), :], x2_send.at[layer])
        wait_for(g1.at[layer, most], g1_send.at[layer])

        @pl.when(layer != s)
        def _():
            wait_for(y1.at[layer], g2_send.at[layer])

        return carry

    lax.fori_loop(0, LAYERS, left, 0)
    for k in range(1, N_SEC):
        wait_for(gain1.at[0], gain_send.at[k])


def widen_kernel(*refs):
    for source, target in zip(refs[:3], refs[3:]):
        target[...] = source[...].astype(F32)


def widen(*values):
    def block(value):
        lead = value.shape[:-1]
        return pl.BlockSpec(
            (*lead, WIDTH // WIDEN_STEPS), lambda n, zeros=(0,) * len(lead): (*zeros, n)
        )

    specs = [block(value) for value in values]
    return pl.pallas_call(
        widen_kernel,
        grid=(WIDEN_STEPS,),
        out_shape=tuple(jax.ShapeDtypeStruct(value.shape, F32) for value in values),
        in_specs=specs,
        out_specs=tuple(specs),
    )(*values)


def body(x_saved, gains, keys, values, grad_top, block_order):
    smem = pl.BlockSpec(memory_space=pltpu.SMEM)
    anywhere = pl.BlockSpec(memory_space=pl.ANY)
    dma = pltpu.SemaphoreType.DMA
    grads, dk, dv = pl.pallas_call(
        kernel,
        out_shape=(
            jax.ShapeDtypeStruct((TOK_DEV, WIDTH), BF16),
            jax.ShapeDtypeStruct((TOK_SEC, WIDTH), BF16),
            jax.ShapeDtypeStruct((TOK_SEC, WIDTH), BF16),
        ),
        in_specs=[smem] + [anywhere] * 5,
        out_specs=(anywhere,) * 3,
        scratch_shapes=[
            pltpu.VMEM((TOK_DEV, WIDE), BF16),
            pltpu.VMEM((TOK_DEV, WIDE), BF16),
            pltpu.VMEM((LAYERS, 2, PART, WIDE), BF16),
            pltpu.VMEM((N_SEC, N_NEAR, PART, HD), BF16),
            pltpu.VMEM((LAYERS, 1, HD), F32),
            pltpu.VMEM((N_NEAR, ROWS, HD), BF16),
            pltpu.VMEM((2, N_NEAR, TOK_DEV, HD), BF16),
            pltpu.VMEM((2, N_NEAR, TOK_DEV, HD), BF16),
            pltpu.VMEM((LAYERS, N_NEAR, ROWS, HD), BF16),
            pltpu.VMEM((NQ, HD), F32),
            pltpu.VMEM((NK, HD), BF16),
            pltpu.VMEM((NK, HD), BF16),
            pltpu.VMEM((HD, NK), BF16),
            pltpu.VMEM((NK, NQ), F32),
            pltpu.VMEM((NK, NQ), F32),
            pltpu.VMEM((NK, NQ), F32),
            pltpu.VMEM((NQ, HD), F32),
            pltpu.VMEM((NK, HD), F32),
            pltpu.VMEM((NK, HD), F32),
            pltpu.VMEM((LAYERS, N_NEAR, ROWS, HD), BF16),
            pltpu.VMEM((LAYERS, TOK_DEV, WIDE), BF16),
        ]
        + [pltpu.VMEM((N_NEAR, TOK_DEV, HD), BF16)] * 8
        + [pltpu.VMEM((TOK_DEV, WIDE), BF16)] * 2
        + [
            dma((16,)),
            dma((15,)),
            dma((N_SEC,)),
            dma((N_SEC,)),
            dma((LAYERS, 2)),
            dma((LAYERS,)),
            dma((LAYERS,)),
            dma((N_SEC,)),
            dma((LAYERS,)),
            dma((LAYERS,)),
            dma((LAYERS,)),
            dma((LAYERS,)),
        ],
        compiler_params=pltpu.CompilerParams(
            vmem_limit_bytes=56 * 2**20, collective_id=0, has_side_effects=True
        ),
    )(block_order, x_saved, gains, keys, values, grad_top)
    return widen(grads[None], dk, dv)


def solution(mesh):
    placed = (
        P("section", "ctx", None),
        P("section", None),
        P(("ctx", "section"), None),
        P(("ctx", "section"), None),
        P("ctx", None),
        P(),
    )
    return jax.shard_map(
        body,
        mesh=mesh,
        in_specs=placed,
        out_specs=(
            P("section", "ctx", None),
            P(("ctx", "section"), None),
            P(("ctx", "section"), None),
        ),
        check_vma=False,
    )
```

```python
import math

import jax
import jax.numpy as jnp
from jax import lax
from jax.experimental import pallas as pl
from jax.experimental.pallas import tpu as pltpu
from jax.sharding import PartitionSpec as P

H = 32
HD = 128
LAYERS = 8
N_SEC = LAYERS
N_CTX = 16
TOK_DEV = 128
WIDTH = H * HD
HEADS_SEC = H // N_SEC
WIDE = HEADS_SEC * HD
N_NEAR = N_CTX // 2
ROWS = TOK_DEV // 2
TOK_SEC = TOK_DEV // N_SEC
NQ = N_NEAR * ROWS
NK = N_CTX * TOK_DEV
PART = ROWS // 2
CHUNKS = (
    (slice(0, 512), 0),
    (slice(512, 1024), 0),
    (slice(1024, 1280), 0),
    (slice(1280, 1536), 128),
    (slice(1536, 1792), 256),
    (slice(1792, 2048), 384),
)
WIDEN_STEPS = 2

masked_score = -1e30
norm_eps = 1e-06
factor = 1.0 / math.sqrt(HD)
log2e = math.log2(math.e)

NT = (((1,), (1,)), ((), ()))
NN = (((1,), (0,)), ((), ()))
BF16, F32 = jnp.bfloat16, jnp.float32


def dot(a, b, dims):
    return lax.dot_general(a, b, dims, preferred_element_type=jnp.float32)


def add_from(total, part, first):
    if total is None:
        return part
    if first == 0:
        return total + part
    return jnp.concatenate([total[:, :first], total[:, first:] + part], axis=1)


def max_from(total, part, first):
    if total is None:
        return part
    if first == 0:
        return jnp.maximum(total, part)
    return jnp.concatenate([total[:, :first], jnp.maximum(total[:, first:], part)], axis=1)


def pick(wanted, options):
    chosen = options[0][1]
    for number, option in options[1:]:
        chosen = lax.select(number == wanted, option, chosen)
    return chosen


def cut(index, size):
    return pl.ds(pl.multiple_of(index * size, size), size)


def kernel(
    place_ref,
    x_hbm,
    gain_hbm,
    keys_hbm,
    values_hbm,
    top_hbm,
    grads_out,
    dk_out,
    dv_out,
    k1,
    v1,
    x1,
    z1,
    gain1,
    top2,
    k2,
    v2,
    x2,
    xw,
    k_ref,
    v_ref,
    kt_ref,
    bias_ref,
    s_ref,
    dp_ref,
    g_ref,
    dk_ref,
    dv_ref,
    g1,
    dk1,
    dv1,
    dk2,
    dv2,
    dk3,
    dv3,
    dk4,
    dv4,
    dk5,
    dv5,
    send,
    recv,
    gain_send,
    gain_recv,
    x1_recv,
    x2_send,
    x2_recv,
    z1_recv,
    z2_recv,
    g1_send,
):
    c, s = lax.axis_index("ctx"), lax.axis_index("section")
    y, x_lo, core = c // 4, (c // 2) % 2, c % 2
    other = 1 - core
    mine, near = y * 2 + core, y * 2 + x_lo

    def device(to_y, to_x_lo, to_core):
        return (to_y * 4 + to_x_lo * 2 + to_core, s)

    def sec_at(k):
        return ((s // 2 + k // 2) % 4) * 2 + (s + k) % 2

    def away(source, target, send_sem, recv_sem, to):
        return pltpu.make_async_remote_copy(
            src_ref=source,
            dst_ref=target,
            send_sem=send_sem,
            recv_sem=recv_sem,
            device_id=to,
            device_id_type=pl.DeviceIdType.MESH,
        )

    def wait_for(ref, sem):
        pltpu.make_async_copy(ref, ref, sem).wait()

    def each(first, last, step):
        def run(k, carry):
            step(k)
            return carry

        lax.fori_loop(first, last, run, 0)

    barrier = pltpu.get_barrier_semaphore()

    def greet(to):
        pl.semaphore_signal(barrier, inc=1, device_id=to, device_id_type=pl.DeviceIdType.MESH)

    each(1, N_SEC, lambda k: greet((c, sec_at(k))))
    each(1, 4, lambda k: greet(device((y + k) % 4, x_lo, core)))
    each(0, 4, lambda k: greet(device((y + k) % 4, x_lo, other)))
    each(0, 4, lambda k: greet(device((y + k) % 4, 1 - x_lo, core)))

    places = [place_ref[b] for b in range(N_CTX)]
    near_places = [place_ref[(e // 2) * 4 + x_lo * 2 + e % 2] for e in range(N_NEAR)]
    ranks = []
    for e in range(N_NEAR):
        rank = 0
        for f in range(N_NEAR):
            if f != e:
                rank = rank + jnp.where(near_places[f] < near_places[e], 1, 0)
        ranks.append(rank)

    def in_order(ref, numbers, target, size, kind):
        blocks = [(number, ref[n]) for n, number in enumerate(numbers)]
        for p in range(len(numbers)):
            target[p * size : (p + 1) * size, :] = pick(p, blocks).astype(kind)

    lane = lax.broadcasted_iota(jnp.int32, (1, NQ), 1)
    query_at = core * ROWS + lane % ROWS
    for e in range(N_NEAR):
        query_at = query_at + jnp.where(lane // ROWS == ranks[e], near_places[e] * TOK_DEV, 0)

    def make_bias(n, carry):
        key_at = lax.broadcasted_iota(jnp.int32, (TOK_DEV, NQ), 0) + n * TOK_DEV
        bias_ref[cut(n, TOK_DEV), :] = jnp.where(key_at <= query_at, 0.0, masked_score)
        return carry

    lax.fori_loop(0, N_CTX, make_bias, 0)
    pl.semaphore_wait(barrier, N_SEC - 1 + 11)

    first_hop = ((keys_hbm, k1), (values_hbm, v1))

    def send_kv1(k):
        to = sec_at(k)
        for n, (source, target) in enumerate(first_hop):
            away(
                source.at[:, cut(to, WIDE)],
                target.at[cut(s, TOK_SEC), :],
                send.at[n],
                recv.at[n],
                (c, to),
            ).start()

    each(1, N_SEC, send_kv1)
    for n, (source, target) in enumerate(first_hop):
        pltpu.make_async_copy(
            source.at[:, cut(s, WIDE)], target.at[cut(s, TOK_SEC), :], recv.at[n]
        ).start()

    def send_gain(k):
        to = sec_at(k)
        away(
            gain_hbm.at[:, cut(to * HEADS_SEC + y, HD)],
            gain1.at[s],
            gain_send.at[k],
            gain_recv.at[s],
            (c, to),
        ).start()

    each(1, N_SEC, send_gain)
    pltpu.make_async_copy(
        gain_hbm.at[:, cut(s * HEADS_SEC + y, HD)], gain1.at[s], gain_recv.at[s]
    ).start()

    for to_core in range(2):
        rows = pl.ds(to_core * ROWS, PART)

        def send_x1(k):
            to = sec_at(k)
            away(
                x_hbm.at[0, rows, cut(to, WIDE)],
                x1.at[s, to_core],
                send.at[2],
                x1_recv.at[s, to_core],
                (c, to),
            ).start()

        each(1, N_SEC, send_x1)
        pltpu.make_async_copy(
            x_hbm.at[0, rows, cut(s, WIDE)], x1.at[s, to_core], x1_recv.at[s, to_core]
        ).start()

    def send_z1(k):
        to_sec = sec_at(k)

        def rows_for(to_y, to_core):
            return x_hbm.at[
                0, pl.ds(to_core * ROWS + PART, PART), cut(to_sec * HEADS_SEC + to_y, HD)
            ]

        def send_to(to_y, to_core):
            away(
                rows_for(to_y, to_core),
                z1.at[to_sec, mine],
                send.at[14],
                z1_recv.at[to_sec],
                device(to_y, x_lo, to_core),
            ).start()

        each(1, 4, lambda q: send_to((y + q) % 4, core))
        each(0, 4, lambda q: send_to((y + q) % 4, other))
        pltpu.make_async_copy(
            rows_for(y, core), z1.at[to_sec, mine], z1_recv.at[to_sec]
        ).start()

    each(1, N_SEC + 1, send_z1)

    def send_top(to_y, to_core):
        away(
            top_hbm.at[cut(to_core, ROWS), cut(s * HEADS_SEC + to_y, HD)],
            top2.at[mine],
            send.at[3],
            recv.at[3],
            device(to_y, x_lo, to_core),
        ).start()

    each(1, 4, lambda k: send_top((y + k) % 4, core))
    each(0, 4, lambda k: send_top((y + k) % 4, other))
    pltpu.make_async_copy(
        top_hbm.at[cut(core, ROWS), cut(s * HEADS_SEC + y, HD)], top2.at[mine], recv.at[3]
    ).start()

    second_hop = ((k1, k2), (v1, v2))
    wait_for(k1, recv.at[0])
    wait_for(v1, recv.at[1])

    def send_kv2(to_y, to_x_lo):
        for n, (source, target) in enumerate(second_hop):
            away(
                source.at[:, cut(to_y, HD)],
                target.at[core, near],
                send.at[4 + n],
                recv.at[4 + n],
                device(to_y, to_x_lo, core),
            ).start()

    each(0, 4, lambda k: send_kv2((y + k) % 4, 1 - x_lo))
    each(1, 4, lambda k: send_kv2((y + k) % 4, x_lo))
    for n, (source, target) in enumerate(second_hop):
        pltpu.make_async_copy(
            source.at[:, cut(y, HD)], target.at[core, near], recv.at[4 + n]
        ).start()

    def pass_z(k):
        to = sec_at(k)
        wait_for(z1.at[to], z1_recv.at[to])
        target = x2.at[s, :, pl.ds(PART, PART), :]

        @pl.when(to != s)
        def _():
            away(z1.at[to], target, send.at[15], z2_recv.at[s], (c, to)).start()

        @pl.when(to == s)
        def _():
            pltpu.make_async_copy(z1.at[to], target, z2_recv.at[s]).start()

    def pass_x(to_core):
        def one(step, carry):
            layer = LAYERS - 1 - step
            wait_for(x1.at[layer, to_core], x1_recv.at[layer, to_core])
            target = x2.at[layer, mine, pl.ds(0, PART), :]

            def send_x2(to_y):
                away(
                    x1.at[layer, to_core, :, cut(to_y, HD)],
                    target,
                    x2_send.at[layer],
                    x2_recv.at[layer],
                    device(to_y, x_lo, to_core),
                ).start()

            each(1, 4, lambda k: send_x2((y + k) % 4))

            @pl.when(core != to_core)
            def _():
                send_x2(y)

            @pl.when(core == to_core)
            def _():
                pltpu.make_async_copy(
                    x1.at[layer, to_core, :, cut(y, HD)], target, x2_recv.at[layer]
                ).start()

            return carry

        lax.fori_loop(0, LAYERS, one, 0)

    pass_x(0)
    each(1, N_SEC + 1, pass_z)
    pass_x(1)

    for n, ref in enumerate((k2, v2)):
        wait_for(ref.at[core], recv.at[4 + n])
        away(
            ref.at[core], ref.at[core], send.at[6 + n], recv.at[6 + n], device(y, x_lo, other)
        ).start()
    wait_for(top2, recv.at[3])
    in_order(top2, ranks, g_ref, ROWS, F32)
    dk_ref[...] = jnp.zeros_like(dk_ref)
    dv_ref[...] = jnp.zeros_like(dv_ref)
    for layer in range(LAYERS):
        wait_for(gain1.at[layer], gain_recv.at[layer])

    wait_for(k2.at[other], recv.at[6])
    wait_for(v2.at[other], recv.at[7])
    for ref, target in ((k2, k_ref), (v2, v_ref)):
        blocks = [(places[b], ref[b % 2, b // 2]) for b in range(N_CTX)]
        for p in range(N_CTX):
            target[p * TOK_DEV : (p + 1) * TOK_DEV, :] = pick(p, blocks)
    for n in range(4):
        rows = slice(n * 512, (n + 1) * 512)
        kt_ref[:, rows] = jnp.transpose(k_ref[rows, :])

    def one_layer(step, carry):
        layer = LAYERS - 1 - step
        wait_for(x2.at[layer, :, pl.ds(0, PART), :], x2_recv.at[layer])
        wait_for(x2.at[layer, :, pl.ds(PART, PART), :], z2_recv.at[layer])
        in_order(x2.at[layer], ranks, xw, ROWS, F32)
        xf = xw[...]
        gain = gain1[layer]
        inv_rms = lax.rsqrt(jnp.mean(xf * xf, axis=1, keepdims=True) + norm_eps)
        query = (xf * inv_rms * gain).astype(BF16)
        grad = g_ref[...].astype(BF16)

        row_max = None
        for rows, first in CHUNKS:
            scores = dot(k_ref[rows, :], query[first:, :], NT) + bias_ref[rows, first:]
            s_ref[rows, first:] = scores
            row_max = max_from(row_max, jnp.max(scores, axis=0, keepdims=True), first)

        total = None
        for rows, first in CHUNKS:
            e = jnp.exp2((s_ref[rows, first:] - row_max[:, first:]) * (factor * log2e))
            s_ref[rows, first:] = e
            total = add_from(total, jnp.sum(e, axis=0, keepdims=True), first)
        inv_total = 1.0 / total

        delta = None
        for rows, first in CHUNKS:
            dp = dot(v_ref[rows, :], grad[first:, :], NT)
            dp_ref[rows, first:] = dp
            probs = s_ref[rows, first:] * inv_total[:, first:]
            s_ref[rows, first:] = probs
            low = probs.astype(BF16)
            part = jnp.sum(low.astype(F32) * dp, axis=0, keepdims=True)
            delta = add_from(delta, part, first)
            dv_ref[rows, :] += dot(low, grad[first:, :], NN)

        dq_t = None
        for rows, first in CHUNKS:
            ds = s_ref[rows, first:] * (dp_ref[rows, first:] - delta[:, first:])
            ds = ds.astype(BF16)
            dk_ref[rows, :] += dot(ds, query[first:, :], NN)
            dq_t = add_from(dq_t, dot(kt_ref[:, rows], ds, NN), first)
        scaled = jnp.transpose(dq_t) * (gain * factor)
        inner = jnp.mean(scaled * xf, axis=1, keepdims=True)
        g_ref[...] += inv_rms * scaled - xf * (inv_rms * inv_rms * inv_rms) * inner
        by_rank = [(r, g_ref[r * ROWS : (r + 1) * ROWS, :].astype(BF16)) for r in range(N_NEAR)]
        for e in range(N_NEAR):
            g1[layer, e] = pick(ranks[e], by_rank)

        target = grads_out.at[cut(core, ROWS), cut(s * HEADS_SEC + y, HD)]

        def send_g(to_y, to_core):
            away(
                g1.at[layer, to_y * 2 + to_core],
                target,
                g1_send.at[layer],
                recv.at[8],
                (to_y * 4 + x_lo * 2 + to_core, layer),
            ).start()

        each(1, 4, lambda k: send_g((y + k) % 4, core))
        each(0, 4, lambda k: send_g((y + k) % 4, other))

        @pl.when(layer != s)
        def _():
            send_g(y, core)

        @pl.when(layer == s)
        def _():
            pltpu.make_async_copy(g1.at[layer, mine], target, recv.at[8]).start()

        return carry

    lax.fori_loop(0, LAYERS, one_layer, 0)

    dk_ref[...] = dk_ref[...] * factor
    sums = (
        (dk_ref, dk1, dk2, dk3, dk4, dk5, dk_out),
        (dv_ref, dv1, dv2, dv3, dv4, dv5, dv_out),
    )

    def in_blocks(ref, of_core, kind):
        by_place = [
            (p, ref[p * TOK_DEV : (p + 1) * TOK_DEV, :].astype(kind)) for p in range(N_CTX)
        ]
        for f in range(N_NEAR):
            yield f, pick(place_ref[f * 2 + of_core], by_place)

    for n, (ref, part1, part2, _, _, _, _) in enumerate(sums):
        for f, rows in in_blocks(ref, other, BF16):
            part1[f] = rows
        away(part1, part2, send.at[8 + n], recv.at[9 + n], device(y, x_lo, other)).start()

    for n, (ref, _, part2, part3, part4, _, _) in enumerate(sums):
        wait_for(part2, recv.at[9 + n])
        for f, rows in in_blocks(ref, core, F32):
            part3[f] = (rows + part2[f].astype(F32)).astype(BF16)

        def send_sum(to_y, to_x_lo):
            away(
                part3.at[to_y * 2 + to_x_lo],
                part4.at[near],
                send.at[10 + n],
                recv.at[11 + n],
                device(to_y, to_x_lo, core),
            ).start()

        each(0, 4, lambda k: send_sum((y + k) % 4, 1 - x_lo))
        each(1, 4, lambda k: send_sum((y + k) % 4, x_lo))
        pltpu.make_async_copy(part3.at[near], part4.at[near], recv.at[11 + n]).start()

    for n, (_, _, _, _, part4, part5, out) in enumerate(sums):
        wait_for(part4, recv.at[11 + n])
        for h in range(HEADS_SEC):
            both = part4[h * 2].astype(F32) + part4[h * 2 + 1].astype(F32)
            part5[:, h * HD : (h + 1) * HD] = both.astype(BF16)

        def send_whole(k):
            to = sec_at(k)
            away(
                part5.at[cut(to, TOK_SEC), :],
                out.at[:, cut(s, WIDE)],
                send.at[12 + n],
                recv.at[13 + n],
                (c, to),
            ).start()

        each(1, N_SEC, send_whole)
        pltpu.make_async_copy(
            part5.at[cut(s, TOK_SEC), :], out.at[:, cut(s, WIDE)], recv.at[13 + n]
        ).start()

    wait_for(grads_out, recv.at[8])
    wait_for(dk_out, recv.at[13])
    wait_for(dv_out, recv.at[14])
    most = pl.ds(0, N_SEC - 1)
    for n, ref in enumerate((k1, v1)):
        wait_for(ref.at[pl.ds(0, TOK_DEV - TOK_SEC), :], send.at[n])
    wait_for(x1.at[most], send.at[2])
    wait_for(z1.at[:, most], send.at[14])
    wait_for(z1.at[most], send.at[15])
    wait_for(top2.at[most], send.at[3])
    for n, ref in enumerate((k2, v2)):
        wait_for(ref.at[0, most], send.at[4 + n])
        wait_for(ref.at[0], send.at[6 + n])
    for n, (_, part1, _, part3, _, part5, _) in enumerate(sums):
        wait_for(part1, send.at[8 + n])
        wait_for(part3.at[most], send.at[10 + n])
        wait_for(part5.at[pl.ds(0, TOK_DEV - TOK_SEC), :], send.at[12 + n])

    def left(layer, carry):
        wait_for(x2.at[layer, most, pl.ds(0, PART), :], x2_send.at[layer])

        @pl.when(layer != s)
        def _():
            wait_for(g1.at[layer], g1_send.at[layer])

        @pl.when(layer == s)
        def _():
            wait_for(g1.at[layer, most], g1_send.at[layer])

        return carry

    lax.fori_loop(0, LAYERS, left, 0)
    for k in range(1, N_SEC):
        wait_for(gain1.at[0], gain_send.at[k])


def widen_kernel(*refs):
    for source, target in zip(refs[:3], refs[3:]):
        target[...] = source[...].astype(F32)


def widen(*values):
    def block(value):
        lead = value.shape[:-1]
        return pl.BlockSpec(
            (*lead, WIDTH // WIDEN_STEPS), lambda n, zeros=(0,) * len(lead): (*zeros, n)
        )

    specs = [block(value) for value in values]
    return pl.pallas_call(
        widen_kernel,
        grid=(WIDEN_STEPS,),
        out_shape=tuple(jax.ShapeDtypeStruct(value.shape, F32) for value in values),
        in_specs=specs,
        out_specs=tuple(specs),
    )(*values)


def body(x_saved, gains, keys, values, grad_top, block_order):
    smem = pl.BlockSpec(memory_space=pltpu.SMEM)
    anywhere = pl.BlockSpec(memory_space=pl.ANY)
    dma = pltpu.SemaphoreType.DMA
    grads, dk, dv = pl.pallas_call(
        kernel,
        out_shape=(
            jax.ShapeDtypeStruct((TOK_DEV, WIDTH), BF16),
            jax.ShapeDtypeStruct((TOK_SEC, WIDTH), BF16),
            jax.ShapeDtypeStruct((TOK_SEC, WIDTH), BF16),
        ),
        in_specs=[smem] + [anywhere] * 5,
        out_specs=(anywhere,) * 3,
        scratch_shapes=[
            pltpu.VMEM((TOK_DEV, WIDE), BF16),
            pltpu.VMEM((TOK_DEV, WIDE), BF16),
            pltpu.VMEM((LAYERS, 2, PART, WIDE), BF16),
            pltpu.VMEM((N_SEC, N_NEAR, PART, HD), BF16),
            pltpu.VMEM((LAYERS, 1, HD), F32),
            pltpu.VMEM((N_NEAR, ROWS, HD), BF16),
            pltpu.VMEM((2, N_NEAR, TOK_DEV, HD), BF16),
            pltpu.VMEM((2, N_NEAR, TOK_DEV, HD), BF16),
            pltpu.VMEM((LAYERS, N_NEAR, ROWS, HD), BF16),
            pltpu.VMEM((NQ, HD), F32),
            pltpu.VMEM((NK, HD), BF16),
            pltpu.VMEM((NK, HD), BF16),
            pltpu.VMEM((HD, NK), BF16),
            pltpu.VMEM((NK, NQ), F32),
            pltpu.VMEM((NK, NQ), F32),
            pltpu.VMEM((NK, NQ), F32),
            pltpu.VMEM((NQ, HD), F32),
            pltpu.VMEM((NK, HD), F32),
            pltpu.VMEM((NK, HD), F32),
            pltpu.VMEM((LAYERS, N_NEAR, ROWS, HD), BF16),
        ]
        + [pltpu.VMEM((N_NEAR, TOK_DEV, HD), BF16)] * 8
        + [pltpu.VMEM((TOK_DEV, WIDE), BF16)] * 2
        + [
            dma((16,)),
            dma((15,)),
            dma((N_SEC,)),
            dma((N_SEC,)),
            dma((LAYERS, 2)),
            dma((LAYERS,)),
            dma((LAYERS,)),
            dma((N_SEC,)),
            dma((LAYERS,)),
            dma((LAYERS,)),
        ],
        compiler_params=pltpu.CompilerParams(
            vmem_limit_bytes=56 * 2**20, collective_id=0, has_side_effects=True
        ),
    )(block_order, x_saved, gains, keys, values, grad_top)
    return widen(grads[None], dk, dv)


def solution(mesh):
    placed = (
        P("section", "ctx", None),
        P("section", None),
        P(("ctx", "section"), None),
        P(("ctx", "section"), None),
        P("ctx", None),
        P(),
    )
    return jax.shard_map(
        body,
        mesh=mesh,
        in_specs=placed,
        out_specs=(
            P("section", "ctx", None),
            P(("ctx", "section"), None),
            P(("ctx", "section"), None),
        ),
        check_vma=False,
    )
```

```python
import math

import jax
import jax.numpy as jnp
from jax import lax
from jax.experimental import pallas as pl
from jax.experimental.pallas import tpu as pltpu
from jax.sharding import PartitionSpec as P

H = 32
HD = 128
LAYERS = 8
N_SEC = LAYERS
N_CTX = 16
TOK_DEV = 128
WIDTH = H * HD
HEADS_SEC = H // N_SEC
WIDE = HEADS_SEC * HD
N_NEAR = N_CTX // 2
ROWS = TOK_DEV // 2
TOK_SEC = TOK_DEV // N_SEC
NQ = N_NEAR * ROWS
NK = N_CTX * TOK_DEV
PART = ROWS // 2
CHUNKS = (
    (slice(0, 512), 0),
    (slice(512, 1024), 0),
    (slice(1024, 1280), 0),
    (slice(1280, 1536), 128),
    (slice(1536, 1792), 256),
    (slice(1792, 2048), 384),
)
TURNS = 2
WIDEN_STEPS = 2

masked_score = -1e30
norm_eps = 1e-06
factor = 1.0 / math.sqrt(HD)
log2e = math.log2(math.e)

NT = (((1,), (1,)), ((), ()))
NN = (((1,), (0,)), ((), ()))
BF16, F32 = jnp.bfloat16, jnp.float32


def dot(a, b, dims):
    return lax.dot_general(a, b, dims, preferred_element_type=jnp.float32)


def add_from(total, part, first):
    if total is None:
        return part
    if first == 0:
        return total + part
    return jnp.concatenate([total[:, :first], total[:, first:] + part], axis=1)


def max_from(total, part, first):
    if total is None:
        return part
    if first == 0:
        return jnp.maximum(total, part)
    return jnp.concatenate([total[:, :first], jnp.maximum(total[:, first:], part)], axis=1)


def pick(wanted, options):
    chosen = options[0][1]
    for number, option in options[1:]:
        chosen = lax.select(number == wanted, option, chosen)
    return chosen


def cut(index, size):
    return pl.ds(pl.multiple_of(index * size, size), size)


def kernel(
    place_ref,
    x_hbm,
    gain_hbm,
    keys_hbm,
    values_hbm,
    top_hbm,
    grads_out,
    dk_out,
    dv_out,
    k1,
    v1,
    x1,
    z1,
    gain1,
    top2,
    k2,
    v2,
    x2,
    xw,
    k_ref,
    v_ref,
    kt_ref,
    bias_ref,
    s_ref,
    dp_ref,
    g_ref,
    dk_ref,
    dv_ref,
    g1,
    dk1,
    dv1,
    dk2,
    dv2,
    dk3,
    dv3,
    dk4,
    dv4,
    dk5,
    dv5,
    dk6,
    dv6,
    send,
    recv,
    gain_send,
    gain_recv,
    x1_recv,
    x2_send,
    x2_recv,
    z1_recv,
    z2_recv,
    g1_send,
):
    c, s = lax.axis_index("ctx"), lax.axis_index("section")
    y, x_lo, core = c // 4, (c // 2) % 2, c % 2
    other = 1 - core
    mine, near = y * 2 + core, y * 2 + x_lo

    def device(to_y, to_x_lo, to_core):
        return (to_y * 4 + to_x_lo * 2 + to_core, s)

    def sec_at(k):
        return ((s // 2 + k // 2) % 4) * 2 + (s + k) % 2

    def away(source, target, send_sem, recv_sem, to):
        return pltpu.make_async_remote_copy(
            src_ref=source,
            dst_ref=target,
            send_sem=send_sem,
            recv_sem=recv_sem,
            device_id=to,
            device_id_type=pl.DeviceIdType.MESH,
        )

    def wait_for(ref, sem):
        pltpu.make_async_copy(ref, ref, sem).wait()

    def each(first, last, step):
        def run(k, carry):
            step(k)
            return carry

        lax.fori_loop(first, last, run, 0)

    barrier = pltpu.get_barrier_semaphore()

    def greet(to):
        pl.semaphore_signal(barrier, inc=1, device_id=to, device_id_type=pl.DeviceIdType.MESH)

    each(1, N_SEC, lambda k: greet((c, sec_at(k))))
    each(1, 4, lambda k: greet(device((y + k) % 4, x_lo, core)))
    each(0, 4, lambda k: greet(device((y + k) % 4, x_lo, other)))
    each(0, 4, lambda k: greet(device((y + k) % 4, 1 - x_lo, core)))

    places = [place_ref[b] for b in range(N_CTX)]
    near_places = [place_ref[(e // 2) * 4 + x_lo * 2 + e % 2] for e in range(N_NEAR)]
    ranks = []
    for e in range(N_NEAR):
        rank = 0
        for f in range(N_NEAR):
            if f != e:
                rank = rank + jnp.where(near_places[f] < near_places[e], 1, 0)
        ranks.append(rank)

    def in_order(ref, numbers, target, size, kind):
        blocks = [(number, ref[n]) for n, number in enumerate(numbers)]
        for p in range(len(numbers)):
            target[p * size : (p + 1) * size, :] = pick(p, blocks).astype(kind)

    lane = lax.broadcasted_iota(jnp.int32, (1, NQ), 1)
    query_at = core * ROWS + lane % ROWS
    for e in range(N_NEAR):
        query_at = query_at + jnp.where(lane // ROWS == ranks[e], near_places[e] * TOK_DEV, 0)

    def make_bias(n, carry):
        key_at = lax.broadcasted_iota(jnp.int32, (TOK_DEV, NQ), 0) + n * TOK_DEV
        bias_ref[cut(n, TOK_DEV), :] = jnp.where(key_at <= query_at, 0.0, masked_score)
        return carry

    lax.fori_loop(0, N_CTX, make_bias, 0)
    pl.semaphore_wait(barrier, N_SEC - 1 + 11)

    first_hop = ((keys_hbm, k1), (values_hbm, v1))

    def send_kv1(k):
        to = sec_at(k)
        for n, (source, target) in enumerate(first_hop):
            away(
                source.at[:, cut(to, WIDE)],
                target.at[cut(s, TOK_SEC), :],
                send.at[n],
                recv.at[n],
                (c, to),
            ).start()

    each(1, N_SEC, send_kv1)
    for n, (source, target) in enumerate(first_hop):
        pltpu.make_async_copy(
            source.at[:, cut(s, WIDE)], target.at[cut(s, TOK_SEC), :], recv.at[n]
        ).start()

    def send_gain(k):
        to = sec_at(k)
        away(
            gain_hbm.at[:, cut(to * HEADS_SEC + y, HD)],
            gain1.at[s],
            gain_send.at[k],
            gain_recv.at[s],
            (c, to),
        ).start()

    each(1, N_SEC, send_gain)
    pltpu.make_async_copy(
        gain_hbm.at[:, cut(s * HEADS_SEC + y, HD)], gain1.at[s], gain_recv.at[s]
    ).start()

    for to_core in range(2):
        rows = pl.ds(to_core * ROWS, PART)

        def send_x1(k):
            to = sec_at(k)
            away(
                x_hbm.at[0, rows, cut(to, WIDE)],
                x1.at[s, to_core],
                send.at[2],
                x1_recv.at[s, to_core],
                (c, to),
            ).start()

        each(1, N_SEC, send_x1)
        pltpu.make_async_copy(
            x_hbm.at[0, rows, cut(s, WIDE)], x1.at[s, to_core], x1_recv.at[s, to_core]
        ).start()

    def send_z1(k):
        to_sec = sec_at(k)

        def rows_for(to_y, to_core):
            return x_hbm.at[
                0, pl.ds(to_core * ROWS + PART, PART), cut(to_sec * HEADS_SEC + to_y, HD)
            ]

        def send_to(to_y, to_core):
            away(
                rows_for(to_y, to_core),
                z1.at[to_sec, mine],
                send.at[14],
                z1_recv.at[to_sec],
                device(to_y, x_lo, to_core),
            ).start()

        each(1, 4, lambda q: send_to((y + q) % 4, core))
        each(0, 4, lambda q: send_to((y + q) % 4, other))
        pltpu.make_async_copy(
            rows_for(y, core), z1.at[to_sec, mine], z1_recv.at[to_sec]
        ).start()

    each(1, N_SEC + 1, send_z1)

    def send_top(to_y, to_core):
        away(
            top_hbm.at[cut(to_core, ROWS), cut(s * HEADS_SEC + to_y, HD)],
            top2.at[mine],
            send.at[3],
            recv.at[3],
            device(to_y, x_lo, to_core),
        ).start()

    each(1, 4, lambda k: send_top((y + k) % 4, core))
    each(0, 4, lambda k: send_top((y + k) % 4, other))
    pltpu.make_async_copy(
        top_hbm.at[cut(core, ROWS), cut(s * HEADS_SEC + y, HD)], top2.at[mine], recv.at[3]
    ).start()

    second_hop = ((k1, k2), (v1, v2))
    wait_for(k1, recv.at[0])
    wait_for(v1, recv.at[1])

    def send_kv2(to_y, to_x_lo):
        for n, (source, target) in enumerate(second_hop):
            away(
                source.at[:, cut(to_y, HD)],
                target.at[core, near],
                send.at[4 + n],
                recv.at[4 + n],
                device(to_y, to_x_lo, core),
            ).start()

    each(0, 4, lambda k: send_kv2((y + k) % 4, 1 - x_lo))
    each(1, 4, lambda k: send_kv2((y + k) % 4, x_lo))
    for n, (source, target) in enumerate(second_hop):
        pltpu.make_async_copy(
            source.at[:, cut(y, HD)], target.at[core, near], recv.at[4 + n]
        ).start()

    def pass_z(k):
        to = sec_at(k)
        wait_for(z1.at[to], z1_recv.at[to])
        target = x2.at[s, :, pl.ds(PART, PART), :]

        @pl.when(to != s)
        def _():
            away(z1.at[to], target, send.at[15], z2_recv.at[s], (c, to)).start()

        @pl.when(to == s)
        def _():
            pltpu.make_async_copy(z1.at[to], target, z2_recv.at[s]).start()

    def pass_x(to_core):
        def one(step, carry):
            layer = LAYERS - 1 - step
            wait_for(x1.at[layer, to_core], x1_recv.at[layer, to_core])
            target = x2.at[layer, mine, pl.ds(0, PART), :]

            def send_x2(to_y):
                away(
                    x1.at[layer, to_core, :, cut(to_y, HD)],
                    target,
                    x2_send.at[layer],
                    x2_recv.at[layer],
                    device(to_y, x_lo, to_core),
                ).start()

            each(1, 4, lambda k: send_x2((y + k) % 4))

            @pl.when(core != to_core)
            def _():
                send_x2(y)

            @pl.when(core == to_core)
            def _():
                pltpu.make_async_copy(
                    x1.at[layer, to_core, :, cut(y, HD)], target, x2_recv.at[layer]
                ).start()

            return carry

        lax.fori_loop(0, LAYERS, one, 0)

    pass_x(0)
    each(1, N_SEC + 1, pass_z)
    pass_x(1)

    for n, ref in enumerate((k2, v2)):
        wait_for(ref.at[core], recv.at[4 + n])
        away(
            ref.at[core], ref.at[core], send.at[6 + n], recv.at[6 + n], device(y, x_lo, other)
        ).start()
    wait_for(top2, recv.at[3])
    in_order(top2, ranks, g_ref, ROWS, F32)
    dk_ref[...] = jnp.zeros_like(dk_ref)
    dv_ref[...] = jnp.zeros_like(dv_ref)
    for layer in range(LAYERS):
        wait_for(gain1.at[layer], gain_recv.at[layer])

    wait_for(k2.at[other], recv.at[6])
    wait_for(v2.at[other], recv.at[7])
    for ref, target in ((k2, k_ref), (v2, v_ref)):
        blocks = [(places[b], ref[b % 2, b // 2]) for b in range(N_CTX)]
        for p in range(N_CTX):
            target[p * TOK_DEV : (p + 1) * TOK_DEV, :] = pick(p, blocks)
    for n in range(4):
        rows = slice(n * 512, (n + 1) * 512)
        kt_ref[:, rows] = jnp.transpose(k_ref[rows, :])

    def wait_layer(layer):
        wait_for(x2.at[layer, :, pl.ds(0, PART), :], x2_recv.at[layer])
        wait_for(x2.at[layer, :, pl.ds(PART, PART), :], z2_recv.at[layer])

    def one_layer(layer, turn):
        in_order(x2.at[layer], ranks, xw.at[turn], ROWS, F32)
        xf = xw[turn]
        gain = gain1[layer]
        inv_rms = lax.rsqrt(jnp.mean(xf * xf, axis=1, keepdims=True) + norm_eps)
        query = (xf * inv_rms * gain).astype(BF16)
        grad = g_ref[...].astype(BF16)

        row_max = None
        for rows, first in CHUNKS:
            scores = dot(k_ref[rows, :], query[first:, :], NT) + bias_ref[rows, first:]
            s_ref[turn, rows, first:] = scores
            row_max = max_from(row_max, jnp.max(scores, axis=0, keepdims=True), first)

        total = None
        for rows, first in CHUNKS:
            e = jnp.exp2((s_ref[turn, rows, first:] - row_max[:, first:]) * (factor * log2e))
            s_ref[turn, rows, first:] = e
            total = add_from(total, jnp.sum(e, axis=0, keepdims=True), first)
        inv_total = 1.0 / total

        delta = None
        for rows, first in CHUNKS:
            dp = dot(v_ref[rows, :], grad[first:, :], NT)
            dp_ref[turn, rows, first:] = dp
            probs = s_ref[turn, rows, first:] * inv_total[:, first:]
            s_ref[turn, rows, first:] = probs
            low = probs.astype(BF16)
            part = jnp.sum(low.astype(F32) * dp, axis=0, keepdims=True)
            delta = add_from(delta, part, first)
            dv_ref[rows, :] += dot(low, grad[first:, :], NN)

        dq_t = None
        for rows, first in CHUNKS:
            ds = s_ref[turn, rows, first:] * (dp_ref[turn, rows, first:] - delta[:, first:])
            ds = ds.astype(BF16)
            dk_ref[rows, :] += dot(ds, query[first:, :], NN)
            dq_t = add_from(dq_t, dot(kt_ref[:, rows], ds, NN), first)
        scaled = jnp.transpose(dq_t) * (gain * factor)
        inner = jnp.mean(scaled * xf, axis=1, keepdims=True)
        g_ref[...] += inv_rms * scaled - xf * (inv_rms * inv_rms * inv_rms) * inner
        by_rank = [(r, g_ref[r * ROWS : (r + 1) * ROWS, :].astype(BF16)) for r in range(N_NEAR)]
        for e in range(N_NEAR):
            g1[layer, e] = pick(ranks[e], by_rank)

    target = grads_out.at[cut(core, ROWS), cut(s * HEADS_SEC + y, HD)]

    def send_g(layer, to_y, to_core):
        away(
            g1.at[layer, to_y * 2 + to_core],
            target,
            g1_send.at[layer],
            recv.at[8],
            (to_y * 4 + x_lo * 2 + to_core, layer),
        ).start()

    def send_layer(layer):
        for k in range(1, 4):
            send_g(layer, (y + k) % 4, core)
        for k in range(4):
            send_g(layer, (y + k) % 4, other)

    def send_own(layer):
        @pl.when(layer != s)
        def _():
            send_g(layer, y, core)

        @pl.when(layer == s)
        def _():
            pltpu.make_async_copy(g1.at[layer, mine], target, recv.at[8]).start()

    def some_layers(step, carry):
        layers = [LAYERS - 1 - step * TURNS - turn for turn in range(TURNS)]
        for layer in layers:
            wait_layer(layer)
        for turn, layer in enumerate(layers):
            one_layer(layer, turn % 2)
        for layer in layers:
            send_layer(layer)
            send_own(layer)
        return carry

    lax.fori_loop(0, LAYERS // TURNS, some_layers, 0)

    dk_ref[...] = dk_ref[...] * factor
    sums = (
        (dk_ref, dk1, dk2, dk3, dk4, dk5, dk6, dk_out),
        (dv_ref, dv1, dv2, dv3, dv4, dv5, dv6, dv_out),
    )

    def by_place(ref, kind):
        return [(p, ref[p * TOK_DEV : (p + 1) * TOK_DEV, :].astype(kind)) for p in range(N_CTX)]

    for n, (ref, part1, part2, _, _, _, _, _) in enumerate(sums):
        rows = by_place(ref, BF16)
        for f in range(N_NEAR):
            part1[f] = pick(place_ref[f * 2 + other], rows)
        away(part1, part2, send.at[8 + n], recv.at[9 + n], device(y, x_lo, other)).start()

    for n, (ref, _, part2, part3, part4, _, _, _) in enumerate(sums):
        wait_for(part2, recv.at[9 + n])
        rows = by_place(ref, F32)
        for to_y in range(4):
            f = to_y * 2 + 1 - x_lo
            both = pick(place_ref[f * 2 + core], rows) + part2[f].astype(F32)
            part3[to_y] = both.astype(BF16)
        away(
            part3, part4, send.at[10 + n], recv.at[11 + n], device(y, 1 - x_lo, core)
        ).start()

    for ref, _, part2, _, _, part5, _, _ in sums:
        rows = by_place(ref, F32)
        for to_y in range(4):
            f = to_y * 2 + x_lo
            part5[to_y] = pick(place_ref[f * 2 + core], rows) + part2[f].astype(F32)

    for n, (_, _, _, _, part4, part5, part6, out) in enumerate(sums):
        wait_for(part4, recv.at[11 + n])
        for to_y in range(4):
            total = part5[to_y] + part4[to_y].astype(F32)
            part6[to_y * TOK_DEV : (to_y + 1) * TOK_DEV, :] = total.astype(BF16)
        target = out.at[:, cut(s * HEADS_SEC + y, HD)]

        def send_sums(k):
            to_sec = sec_at(k)

            def send_sum(to_y):
                away(
                    part6.at[cut(to_y * N_SEC + to_sec, TOK_SEC), :],
                    target,
                    send.at[12 + n],
                    recv.at[13 + n],
                    (to_y * 4 + x_lo * 2 + core, to_sec),
                ).start()

            each(1, 4, lambda q: send_sum((y + q) % 4))

            @pl.when(to_sec != s)
            def _():
                send_sum(y)

            @pl.when(to_sec == s)
            def _():
                pltpu.make_async_copy(
                    part6.at[cut(y * N_SEC + s, TOK_SEC), :], target, recv.at[13 + n]
                ).start()

        each(1, N_SEC + 1, send_sums)

    wait_for(grads_out, recv.at[8])
    wait_for(dk_out, recv.at[13])
    wait_for(dv_out, recv.at[14])
    most = pl.ds(0, N_SEC - 1)
    for n, ref in enumerate((k1, v1)):
        wait_for(ref.at[pl.ds(0, TOK_DEV - TOK_SEC), :], send.at[n])
    wait_for(x1.at[most], send.at[2])
    wait_for(z1.at[:, most], send.at[14])
    wait_for(z1.at[most], send.at[15])
    wait_for(top2.at[most], send.at[3])
    for n, ref in enumerate((k2, v2)):
        wait_for(ref.at[0, most], send.at[4 + n])
        wait_for(ref.at[0], send.at[6 + n])
    for n, (_, part1, _, part3, _, _, part6, _) in enumerate(sums):
        wait_for(part1, send.at[8 + n])
        wait_for(part3, send.at[10 + n])
        wait_for(part6.at[pl.ds(0, 4 * TOK_DEV - TOK_SEC), :], send.at[12 + n])

    def left(layer, carry):
        wait_for(x2.at[layer, most, pl.ds(0, PART), :], x2_send.at[layer])

        @pl.when(layer != s)
        def _():
            wait_for(g1.at[layer], g1_send.at[layer])

        @pl.when(layer == s)
        def _():
            wait_for(g1.at[layer, most], g1_send.at[layer])

        return carry

    lax.fori_loop(0, LAYERS, left, 0)
    for k in range(1, N_SEC):
        wait_for(gain1.at[0], gain_send.at[k])


def widen_kernel(*refs):
    for source, target in zip(refs[:3], refs[3:]):
        target[...] = source[...].astype(F32)


def widen(*values):
    def block(value):
        lead = value.shape[:-1]
        return pl.BlockSpec(
            (*lead, WIDTH // WIDEN_STEPS), lambda n, zeros=(0,) * len(lead): (*zeros, n)
        )

    specs = [block(value) for value in values]
    return pl.pallas_call(
        widen_kernel,
        grid=(WIDEN_STEPS,),
        out_shape=tuple(jax.ShapeDtypeStruct(value.shape, F32) for value in values),
        in_specs=specs,
        out_specs=tuple(specs),
    )(*values)


def body(x_saved, gains, keys, values, grad_top, block_order):
    smem = pl.BlockSpec(memory_space=pltpu.SMEM)
    anywhere = pl.BlockSpec(memory_space=pl.ANY)
    dma = pltpu.SemaphoreType.DMA
    grads, dk, dv = pl.pallas_call(
        kernel,
        out_shape=(
            jax.ShapeDtypeStruct((TOK_DEV, WIDTH), BF16),
            jax.ShapeDtypeStruct((TOK_SEC, WIDTH), BF16),
            jax.ShapeDtypeStruct((TOK_SEC, WIDTH), BF16),
        ),
        in_specs=[smem] + [anywhere] * 5,
        out_specs=(anywhere,) * 3,
        scratch_shapes=[
            pltpu.VMEM((TOK_DEV, WIDE), BF16),
            pltpu.VMEM((TOK_DEV, WIDE), BF16),
            pltpu.VMEM((LAYERS, 2, PART, WIDE), BF16),
            pltpu.VMEM((N_SEC, N_NEAR, PART, HD), BF16),
            pltpu.VMEM((LAYERS, 1, HD), F32),
            pltpu.VMEM((N_NEAR, ROWS, HD), BF16),
            pltpu.VMEM((2, N_NEAR, TOK_DEV, HD), BF16),
            pltpu.VMEM((2, N_NEAR, TOK_DEV, HD), BF16),
            pltpu.VMEM((LAYERS, N_NEAR, ROWS, HD), BF16),
            pltpu.VMEM((2, NQ, HD), F32),
            pltpu.VMEM((NK, HD), BF16),
            pltpu.VMEM((NK, HD), BF16),
            pltpu.VMEM((HD, NK), BF16),
            pltpu.VMEM((NK, NQ), F32),
            pltpu.VMEM((2, NK, NQ), F32),
            pltpu.VMEM((2, NK, NQ), F32),
            pltpu.VMEM((NQ, HD), F32),
            pltpu.VMEM((NK, HD), F32),
            pltpu.VMEM((NK, HD), F32),
            pltpu.VMEM((LAYERS, N_NEAR, ROWS, HD), BF16),
        ]
        + [pltpu.VMEM((N_NEAR, TOK_DEV, HD), BF16)] * 4
        + [pltpu.VMEM((4, TOK_DEV, HD), BF16)] * 4
        + [pltpu.VMEM((4, TOK_DEV, HD), F32)] * 2
        + [pltpu.VMEM((4 * TOK_DEV, HD), BF16)] * 2
        + [
            dma((16,)),
            dma((15,)),
            dma((N_SEC,)),
            dma((N_SEC,)),
            dma((LAYERS, 2)),
            dma((LAYERS,)),
            dma((LAYERS,)),
            dma((N_SEC,)),
            dma((LAYERS,)),
            dma((LAYERS,)),
        ],
        compiler_params=pltpu.CompilerParams(
            vmem_limit_bytes=56 * 2**20, collective_id=0, has_side_effects=True
        ),
    )(block_order, x_saved, gains, keys, values, grad_top)
    return widen(grads[None], dk, dv)


def solution(mesh):
    placed = (
        P("section", "ctx", None),
        P("section", None),
        P(("ctx", "section"), None),
        P(("ctx", "section"), None),
        P("ctx", None),
        P(),
    )
    return jax.shard_map(
        body,
        mesh=mesh,
        in_specs=placed,
        out_specs=(
            P("section", "ctx", None),
            P(("ctx", "section"), None),
            P(("ctx", "section"), None),
        ),
        check_vma=False,
    )
```

```python
import math

import jax
import jax.numpy as jnp
from jax import lax
from jax.experimental import pallas as pl
from jax.experimental.pallas import tpu as pltpu
from jax.sharding import PartitionSpec as P

H = 32
HD = 128
LAYERS = 8
N_SEC = LAYERS
N_CTX = 16
TOK_DEV = 128
WIDTH = H * HD
HEADS_SEC = H // N_SEC
WIDE = HEADS_SEC * HD
N_NEAR = N_CTX // 2
ROWS = TOK_DEV // 2
TOK_SEC = TOK_DEV // N_SEC
NQ = N_NEAR * ROWS
NK = N_CTX * TOK_DEV
PART = ROWS // 2
CHUNKS = (
    (slice(0, 512), 0),
    (slice(512, 1024), 0),
    (slice(1024, 1280), 0),
    (slice(1280, 1536), 128),
    (slice(1536, 1792), 256),
    (slice(1792, 2048), 384),
)
TURNS = 2
WIDEN_STEPS = 2

masked_score = -1e30
norm_eps = 1e-06
factor = 1.0 / math.sqrt(HD)
log2e = math.log2(math.e)

NT = (((1,), (1,)), ((), ()))
NN = (((1,), (0,)), ((), ()))
BF16, F32 = jnp.bfloat16, jnp.float32


def dot(a, b, dims):
    return lax.dot_general(a, b, dims, preferred_element_type=jnp.float32)


def add_from(total, part, first):
    if total is None:
        return part
    if first == 0:
        return total + part
    return jnp.concatenate([total[:, :first], total[:, first:] + part], axis=1)


def max_from(total, part, first):
    if total is None:
        return part
    if first == 0:
        return jnp.maximum(total, part)
    return jnp.concatenate([total[:, :first], jnp.maximum(total[:, first:], part)], axis=1)


def pick(wanted, options):
    chosen = options[0][1]
    for number, option in options[1:]:
        chosen = lax.select(number == wanted, option, chosen)
    return chosen


def cut(index, size):
    return pl.ds(pl.multiple_of(index * size, size), size)


def kernel(
    place_ref,
    x_hbm,
    gain_hbm,
    keys_hbm,
    values_hbm,
    top_hbm,
    grads_out,
    dk_out,
    dv_out,
    k1,
    v1,
    x1,
    z1,
    gain1,
    top2,
    k2,
    v2,
    x2,
    xw,
    k_ref,
    v_ref,
    kt_ref,
    bias_ref,
    s_ref,
    dp_ref,
    g_ref,
    dk_ref,
    dv_ref,
    g1,
    dk1,
    dv1,
    dk2,
    dv2,
    dk3,
    dv3,
    dk4,
    dv4,
    dk5,
    dv5,
    dk6,
    dv6,
    send,
    recv,
    gain_send,
    gain_recv,
    x1_recv,
    x2_send,
    x2_recv,
    z1_recv,
    z2_recv,
    g1_send,
):
    c, s = lax.axis_index("ctx"), lax.axis_index("section")
    y, x_lo, core = c // 4, (c // 2) % 2, c % 2
    other = 1 - core
    mine, near = y * 2 + core, y * 2 + x_lo

    def device(to_y, to_x_lo, to_core):
        return (to_y * 4 + to_x_lo * 2 + to_core, s)

    def sec_at(k):
        return ((s // 2 + k // 2) % 4) * 2 + (s + k) % 2

    def away(source, target, send_sem, recv_sem, to):
        return pltpu.make_async_remote_copy(
            src_ref=source,
            dst_ref=target,
            send_sem=send_sem,
            recv_sem=recv_sem,
            device_id=to,
            device_id_type=pl.DeviceIdType.MESH,
        )

    def wait_for(ref, sem):
        pltpu.make_async_copy(ref, ref, sem).wait()

    def each(first, last, step):
        def run(k, carry):
            step(k)
            return carry

        lax.fori_loop(first, last, run, 0)

    barrier = pltpu.get_barrier_semaphore()

    def greet(to):
        pl.semaphore_signal(barrier, inc=1, device_id=to, device_id_type=pl.DeviceIdType.MESH)

    each(1, N_SEC, lambda k: greet((c, sec_at(k))))
    each(1, 4, lambda k: greet(device((y + k) % 4, x_lo, core)))
    each(0, 4, lambda k: greet(device((y + k) % 4, x_lo, other)))
    each(0, 4, lambda k: greet(device((y + k) % 4, 1 - x_lo, core)))

    places = [place_ref[b] for b in range(N_CTX)]
    near_places = [place_ref[(e // 2) * 4 + x_lo * 2 + e % 2] for e in range(N_NEAR)]
    ranks = []
    for e in range(N_NEAR):
        rank = 0
        for f in range(N_NEAR):
            if f != e:
                rank = rank + jnp.where(near_places[f] < near_places[e], 1, 0)
        ranks.append(rank)

    def in_order(ref, numbers, target, size, kind):
        blocks = [(number, ref[n]) for n, number in enumerate(numbers)]
        for p in range(len(numbers)):
            target[p * size : (p + 1) * size, :] = pick(p, blocks).astype(kind)

    lane = lax.broadcasted_iota(jnp.int32, (1, NQ), 1)
    query_at = core * ROWS + lane % ROWS
    for e in range(N_NEAR):
        query_at = query_at + jnp.where(lane // ROWS == ranks[e], near_places[e] * TOK_DEV, 0)

    def make_bias(n, carry):
        key_at = lax.broadcasted_iota(jnp.int32, (TOK_DEV, NQ), 0) + n * TOK_DEV
        bias_ref[cut(n, TOK_DEV), :] = jnp.where(key_at <= query_at, 0.0, masked_score)
        return carry

    lax.fori_loop(0, N_CTX, make_bias, 0)
    pl.semaphore_wait(barrier, N_SEC - 1 + 11)

    first_hop = ((keys_hbm, k1), (values_hbm, v1))

    def send_kv1(k):
        to = sec_at(k)
        for n, (source, target) in enumerate(first_hop):
            away(
                source.at[:, cut(to, WIDE)],
                target.at[cut(s, TOK_SEC), :],
                send.at[n],
                recv.at[n],
                (c, to),
            ).start()

    each(1, N_SEC, send_kv1)
    for n, (source, target) in enumerate(first_hop):
        pltpu.make_async_copy(
            source.at[:, cut(s, WIDE)], target.at[cut(s, TOK_SEC), :], recv.at[n]
        ).start()

    def send_gain(k):
        to = sec_at(k)
        away(
            gain_hbm.at[:, cut(to * HEADS_SEC + y, HD)],
            gain1.at[s],
            gain_send.at[k],
            gain_recv.at[s],
            (c, to),
        ).start()

    each(1, N_SEC, send_gain)
    pltpu.make_async_copy(
        gain_hbm.at[:, cut(s * HEADS_SEC + y, HD)], gain1.at[s], gain_recv.at[s]
    ).start()

    for to_core in range(2):
        rows = pl.ds(to_core * ROWS, PART)

        def send_x1(k):
            to = sec_at(k)
            away(
                x_hbm.at[0, rows, cut(to, WIDE)],
                x1.at[s, to_core],
                send.at[2],
                x1_recv.at[s, to_core],
                (c, to),
            ).start()

        each(1, N_SEC, send_x1)
        pltpu.make_async_copy(
            x_hbm.at[0, rows, cut(s, WIDE)], x1.at[s, to_core], x1_recv.at[s, to_core]
        ).start()

    def send_z1(k):
        to_sec = sec_at(k)

        def rows_for(to_y, to_core):
            return x_hbm.at[
                0, pl.ds(to_core * ROWS + PART, PART), cut(to_sec * HEADS_SEC + to_y, HD)
            ]

        def send_to(to_y, to_core):
            away(
                rows_for(to_y, to_core),
                z1.at[to_sec, mine],
                send.at[14],
                z1_recv.at[to_sec],
                device(to_y, x_lo, to_core),
            ).start()

        each(1, 4, lambda q: send_to((y + q) % 4, core))
        each(0, 4, lambda q: send_to((y + q) % 4, other))
        pltpu.make_async_copy(
            rows_for(y, core), z1.at[to_sec, mine], z1_recv.at[to_sec]
        ).start()

    each(1, N_SEC + 1, send_z1)

    def send_top(to_y, to_core):
        away(
            top_hbm.at[cut(to_core, ROWS), cut(s * HEADS_SEC + to_y, HD)],
            top2.at[mine],
            send.at[3],
            recv.at[3],
            device(to_y, x_lo, to_core),
        ).start()

    each(1, 4, lambda k: send_top((y + k) % 4, core))
    each(0, 4, lambda k: send_top((y + k) % 4, other))
    pltpu.make_async_copy(
        top_hbm.at[cut(core, ROWS), cut(s * HEADS_SEC + y, HD)], top2.at[mine], recv.at[3]
    ).start()

    second_hop = ((k1, k2), (v1, v2))
    wait_for(k1, recv.at[0])
    wait_for(v1, recv.at[1])

    def send_kv2(to_y, to_x_lo):
        for n, (source, target) in enumerate(second_hop):
            away(
                source.at[:, cut(to_y, HD)],
                target.at[core, near],
                send.at[4 + n],
                recv.at[4 + n],
                device(to_y, to_x_lo, core),
            ).start()

    each(0, 4, lambda k: send_kv2((y + k) % 4, 1 - x_lo))
    each(1, 4, lambda k: send_kv2((y + k) % 4, x_lo))
    for n, (source, target) in enumerate(second_hop):
        pltpu.make_async_copy(
            source.at[:, cut(y, HD)], target.at[core, near], recv.at[4 + n]
        ).start()

    def pass_z(k):
        to = sec_at(k)
        wait_for(z1.at[to], z1_recv.at[to])
        target = x2.at[s, :, pl.ds(PART, PART), :]

        @pl.when(to != s)
        def _():
            away(z1.at[to], target, send.at[15], z2_recv.at[s], (c, to)).start()

        @pl.when(to == s)
        def _():
            pltpu.make_async_copy(z1.at[to], target, z2_recv.at[s]).start()

    def pass_x(to_core):
        def one(step, carry):
            layer = LAYERS - 1 - step
            wait_for(x1.at[layer, to_core], x1_recv.at[layer, to_core])
            target = x2.at[layer, mine, pl.ds(0, PART), :]

            def send_x2(to_y):
                away(
                    x1.at[layer, to_core, :, cut(to_y, HD)],
                    target,
                    x2_send.at[layer],
                    x2_recv.at[layer],
                    device(to_y, x_lo, to_core),
                ).start()

            each(1, 4, lambda k: send_x2((y + k) % 4))

            @pl.when(core != to_core)
            def _():
                send_x2(y)

            @pl.when(core == to_core)
            def _():
                pltpu.make_async_copy(
                    x1.at[layer, to_core, :, cut(y, HD)], target, x2_recv.at[layer]
                ).start()

            return carry

        lax.fori_loop(0, LAYERS, one, 0)

    pass_x(0)
    each(1, N_SEC + 1, pass_z)
    pass_x(1)

    for n, ref in enumerate((k2, v2)):
        wait_for(ref.at[core], recv.at[4 + n])
        away(
            ref.at[core], ref.at[core], send.at[6 + n], recv.at[6 + n], device(y, x_lo, other)
        ).start()
    wait_for(top2, recv.at[3])
    in_order(top2, ranks, g_ref, ROWS, F32)
    dk_ref[...] = jnp.zeros_like(dk_ref)
    dv_ref[...] = jnp.zeros_like(dv_ref)
    for layer in range(LAYERS):
        wait_for(gain1.at[layer], gain_recv.at[layer])

    wait_for(k2.at[other], recv.at[6])
    wait_for(v2.at[other], recv.at[7])
    for ref, target in ((k2, k_ref), (v2, v_ref)):
        blocks = [(places[b], ref[b % 2, b // 2]) for b in range(N_CTX)]
        for p in range(N_CTX):
            target[p * TOK_DEV : (p + 1) * TOK_DEV, :] = pick(p, blocks)
    for n in range(4):
        rows = slice(n * 512, (n + 1) * 512)
        kt_ref[:, rows] = jnp.transpose(k_ref[rows, :])

    def wait_layer(layer):
        wait_for(x2.at[layer, :, pl.ds(0, PART), :], x2_recv.at[layer])
        wait_for(x2.at[layer, :, pl.ds(PART, PART), :], z2_recv.at[layer])

    def one_layer(layer, turn):
        in_order(x2.at[layer], ranks, xw.at[turn], ROWS, F32)
        xf = xw[turn]
        gain = gain1[layer]
        inv_rms = lax.rsqrt(jnp.mean(xf * xf, axis=1, keepdims=True) + norm_eps)
        query = (xf * inv_rms * gain).astype(BF16)
        grad = g_ref[...].astype(BF16)

        row_max = None
        for rows, first in CHUNKS:
            scores = dot(k_ref[rows, :], query[first:, :], NT) + bias_ref[rows, first:]
            s_ref[turn, rows, first:] = scores
            row_max = max_from(row_max, jnp.max(scores, axis=0, keepdims=True), first)

        total = None
        for rows, first in CHUNKS:
            e = jnp.exp2((s_ref[turn, rows, first:] - row_max[:, first:]) * (factor * log2e))
            s_ref[turn, rows, first:] = e
            total = add_from(total, jnp.sum(e, axis=0, keepdims=True), first)
        inv_total = 1.0 / total

        delta = None
        for rows, first in CHUNKS:
            dp = dot(v_ref[rows, :], grad[first:, :], NT)
            dp_ref[turn, rows, first:] = dp
            probs = s_ref[turn, rows, first:] * inv_total[:, first:]
            s_ref[turn, rows, first:] = probs
            low = probs.astype(BF16)
            part = jnp.sum(low.astype(F32) * dp, axis=0, keepdims=True)
            delta = add_from(delta, part, first)
            dv_ref[rows, :] += dot(low, grad[first:, :], NN)

        dq_t = None
        for rows, first in CHUNKS:
            ds = s_ref[turn, rows, first:] * (dp_ref[turn, rows, first:] - delta[:, first:])
            ds = ds.astype(BF16)
            dk_ref[rows, :] += dot(ds, query[first:, :], NN)
            dq_t = add_from(dq_t, dot(kt_ref[:, rows], ds, NN), first)
        scaled = jnp.transpose(dq_t) * (gain * factor)
        inner = jnp.mean(scaled * xf, axis=1, keepdims=True)
        g_ref[...] += inv_rms * scaled - xf * (inv_rms * inv_rms * inv_rms) * inner
        by_rank = [(r, g_ref[r * ROWS : (r + 1) * ROWS, :].astype(BF16)) for r in range(N_NEAR)]
        for e in range(N_NEAR):
            g1[layer, e] = pick(ranks[e], by_rank)

    target = grads_out.at[cut(core, ROWS), cut(s * HEADS_SEC + y, HD)]

    def send_g(layer, to_y, to_core):
        away(
            g1.at[layer, to_y * 2 + to_core],
            target,
            g1_send.at[layer],
            recv.at[8],
            (to_y * 4 + x_lo * 2 + to_core, layer),
        ).start()

    def send_layer(layer):
        for k in range(1, 4):
            send_g(layer, (y + k) % 4, core)
        for k in range(4):
            send_g(layer, (y + k) % 4, other)

    def send_own(layer):
        @pl.when(layer != s)
        def _():
            send_g(layer, y, core)

        @pl.when(layer == s)
        def _():
            pltpu.make_async_copy(g1.at[layer, mine], target, recv.at[8]).start()

    def some_layers(step, carry):
        layers = [LAYERS - 1 - step * TURNS - turn for turn in range(TURNS)]
        for layer in layers:
            wait_layer(layer)
        for turn, layer in enumerate(layers):
            one_layer(layer, turn % 2)
        for layer in layers:
            send_layer(layer)
        for layer in layers:
            send_own(layer)
        return carry

    lax.fori_loop(0, LAYERS // TURNS, some_layers, 0)

    sums = (
        (dv_ref, dv1, dv2, dv3, dv4, dv5, dv6, dv_out),
        (dk_ref, dk1, dk2, dk3, dk4, dk5, dk6, dk_out),
    )

    def by_place(ref, kind):
        scale = factor if ref is dk_ref else 1.0
        return [
            (p, (ref[p * TOK_DEV : (p + 1) * TOK_DEV, :] * scale).astype(kind))
            for p in range(N_CTX)
        ]

    for n, (ref, part1, part2, _, _, _, _, _) in enumerate(sums):
        rows = by_place(ref, BF16)
        for f in range(N_NEAR):
            part1[f] = pick(place_ref[f * 2 + other], rows)
        away(part1, part2, send.at[8 + n], recv.at[9 + n], device(y, x_lo, other)).start()

    for n, (ref, _, part2, part3, part4, _, _, _) in enumerate(sums):
        wait_for(part2, recv.at[9 + n])
        rows = by_place(ref, F32)
        for to_y in range(4):
            f = to_y * 2 + 1 - x_lo
            both = pick(place_ref[f * 2 + core], rows) + part2[f].astype(F32)
            part3[to_y] = both.astype(BF16)
        away(
            part3, part4, send.at[10 + n], recv.at[11 + n], device(y, 1 - x_lo, core)
        ).start()

    for ref, _, part2, _, _, part5, _, _ in sums:
        rows = by_place(ref, F32)
        for to_y in range(4):
            f = to_y * 2 + x_lo
            part5[to_y] = pick(place_ref[f * 2 + core], rows) + part2[f].astype(F32)

    for n, (_, _, _, _, part4, part5, part6, out) in enumerate(sums):
        wait_for(part4, recv.at[11 + n])
        for to_y in range(4):
            total = part5[to_y] + part4[to_y].astype(F32)
            part6[to_y * TOK_DEV : (to_y + 1) * TOK_DEV, :] = total.astype(BF16)
        target = out.at[:, cut(s * HEADS_SEC + y, HD)]

        def send_sums(k):
            to_sec = sec_at(k)

            def send_sum(to_y):
                away(
                    part6.at[cut(to_y * N_SEC + to_sec, TOK_SEC), :],
                    target,
                    send.at[12 + n],
                    recv.at[13 + n],
                    (to_y * 4 + x_lo * 2 + core, to_sec),
                ).start()

            each(1, 4, lambda q: send_sum((y + q) % 4))

            @pl.when(to_sec != s)
            def _():
                send_sum(y)

            @pl.when(to_sec == s)
            def _():
                pltpu.make_async_copy(
                    part6.at[cut(y * N_SEC + s, TOK_SEC), :], target, recv.at[13 + n]
                ).start()

        each(1, N_SEC + 1, send_sums)

    wait_for(grads_out, recv.at[8])
    wait_for(dv_out, recv.at[13])
    wait_for(dk_out, recv.at[14])
    most = pl.ds(0, N_SEC - 1)
    for n, ref in enumerate((k1, v1)):
        wait_for(ref.at[pl.ds(0, TOK_DEV - TOK_SEC), :], send.at[n])
    wait_for(x1.at[most], send.at[2])
    wait_for(z1.at[:, most], send.at[14])
    wait_for(z1.at[most], send.at[15])
    wait_for(top2.at[most], send.at[3])
    for n, ref in enumerate((k2, v2)):
        wait_for(ref.at[0, most], send.at[4 + n])
        wait_for(ref.at[0], send.at[6 + n])
    for n, (_, part1, _, part3, _, _, part6, _) in enumerate(sums):
        wait_for(part1, send.at[8 + n])
        wait_for(part3, send.at[10 + n])
        wait_for(part6.at[pl.ds(0, 4 * TOK_DEV - TOK_SEC), :], send.at[12 + n])

    def left(layer, carry):
        wait_for(x2.at[layer, most, pl.ds(0, PART), :], x2_send.at[layer])

        @pl.when(layer != s)
        def _():
            wait_for(g1.at[layer], g1_send.at[layer])

        @pl.when(layer == s)
        def _():
            wait_for(g1.at[layer, most], g1_send.at[layer])

        return carry

    lax.fori_loop(0, LAYERS, left, 0)
    for k in range(1, N_SEC):
        wait_for(gain1.at[0], gain_send.at[k])


def widen_kernel(*refs):
    for source, target in zip(refs[:3], refs[3:]):
        target[...] = source[...].astype(F32)


def widen(*values):
    def block(value):
        lead = value.shape[:-1]
        return pl.BlockSpec(
            (*lead, WIDTH // WIDEN_STEPS), lambda n, zeros=(0,) * len(lead): (*zeros, n)
        )

    specs = [block(value) for value in values]
    return pl.pallas_call(
        widen_kernel,
        grid=(WIDEN_STEPS,),
        out_shape=tuple(jax.ShapeDtypeStruct(value.shape, F32) for value in values),
        in_specs=specs,
        out_specs=tuple(specs),
    )(*values)


def body(x_saved, gains, keys, values, grad_top, block_order):
    smem = pl.BlockSpec(memory_space=pltpu.SMEM)
    anywhere = pl.BlockSpec(memory_space=pl.ANY)
    dma = pltpu.SemaphoreType.DMA
    grads, dk, dv = pl.pallas_call(
        kernel,
        out_shape=(
            jax.ShapeDtypeStruct((TOK_DEV, WIDTH), BF16),
            jax.ShapeDtypeStruct((TOK_SEC, WIDTH), BF16),
            jax.ShapeDtypeStruct((TOK_SEC, WIDTH), BF16),
        ),
        in_specs=[smem] + [anywhere] * 5,
        out_specs=(anywhere,) * 3,
        scratch_shapes=[
            pltpu.VMEM((TOK_DEV, WIDE), BF16),
            pltpu.VMEM((TOK_DEV, WIDE), BF16),
            pltpu.VMEM((LAYERS, 2, PART, WIDE), BF16),
            pltpu.VMEM((N_SEC, N_NEAR, PART, HD), BF16),
            pltpu.VMEM((LAYERS, 1, HD), F32),
            pltpu.VMEM((N_NEAR, ROWS, HD), BF16),
            pltpu.VMEM((2, N_NEAR, TOK_DEV, HD), BF16),
            pltpu.VMEM((2, N_NEAR, TOK_DEV, HD), BF16),
            pltpu.VMEM((LAYERS, N_NEAR, ROWS, HD), BF16),
            pltpu.VMEM((2, NQ, HD), F32),
            pltpu.VMEM((NK, HD), BF16),
            pltpu.VMEM((NK, HD), BF16),
            pltpu.VMEM((HD, NK), BF16),
            pltpu.VMEM((NK, NQ), F32),
            pltpu.VMEM((2, NK, NQ), F32),
            pltpu.VMEM((2, NK, NQ), F32),
            pltpu.VMEM((NQ, HD), F32),
            pltpu.VMEM((NK, HD), F32),
            pltpu.VMEM((NK, HD), F32),
            pltpu.VMEM((LAYERS, N_NEAR, ROWS, HD), BF16),
        ]
        + [pltpu.VMEM((N_NEAR, TOK_DEV, HD), BF16)] * 4
        + [pltpu.VMEM((4, TOK_DEV, HD), BF16)] * 4
        + [pltpu.VMEM((4, TOK_DEV, HD), F32)] * 2
        + [pltpu.VMEM((4 * TOK_DEV, HD), BF16)] * 2
        + [
            dma((16,)),
            dma((15,)),
            dma((N_SEC,)),
            dma((N_SEC,)),
            dma((LAYERS, 2)),
            dma((LAYERS,)),
            dma((LAYERS,)),
            dma((N_SEC,)),
            dma((LAYERS,)),
            dma((LAYERS,)),
        ],
        compiler_params=pltpu.CompilerParams(
            vmem_limit_bytes=56 * 2**20, collective_id=0, has_side_effects=True
        ),
    )(block_order, x_saved, gains, keys, values, grad_top)
    return widen(grads[None], dk, dv)


def solution(mesh):
    placed = (
        P("section", "ctx", None),
        P("section", None),
        P(("ctx", "section"), None),
        P(("ctx", "section"), None),
        P("ctx", None),
        P(),
    )
    return jax.shard_map(
        body,
        mesh=mesh,
        in_specs=placed,
        out_specs=(
            P("section", "ctx", None),
            P(("ctx", "section"), None),
            P(("ctx", "section"), None),
        ),
        check_vma=False,
    )
```
